32 devices in a mesh: groups: 2 (over y), outer: 4 (over z), inner: 4 (over x, core).
Axes of the slice: x: 2, y: 2, z: 4, core: 2. Of those that a mesh axis runs over, the one named last changes fastest.
Arguments:
- decoder: bfloat16 [4096, 16384], P('inner', ('groups', 'outer')), parts along dimension 1, may hold values from -0.09375 to 0.09375
- stretch_blocks: int32 [64, 2], P('groups'), parts along dimension 0, may hold values from 0 to 63, as said below
- stretch_weight: float32 [64], P('groups'), parts along dimension 0, may hold values from 24 to 192
Outputs:
- tangent_grad: bfloat16 [4096, 16384], P('inner', ('groups', 'outer')), parts along dimension 1
The draws below stay inside these ranges and needn't reach their ends.
There are 2 independent parts, one for each index of `groups`. The reference program is written for one: setup_inputs(seed, part) draws one part's arguments, and reference() takes and returns one part's arrays. A program takes and returns all parts, laid end to end along the dimension named above; each array names one. Nothing has to cross between parts.
Inputs may be any that keep to these rules, and one draw needn't show every extreme that they name: `stretch_blocks`: each block id appears once. Block b is stored at outer index b // 16. Stretches c with equal c // 8 form one group of 16 blocks; at each outer index either exactly 4 or none of a group's blocks are stored. The second block of every stretch is stored 2 outer indices below its first block, counted around the axis, so every outer index stores the first blocks of 8 stretches.
All inputs are finite; a program needn't handle non-finite values.
Results may differ from the reference program's by a relative error of at most 0.0085.
Values may be sent and summed in bfloat16 or wider, within the bound.
No kernel may reach another device: no remote copies, remote signals or barrier semaphores. Data moves between devices by JAX's collectives and lax.ppermute only.
A program may use at most 64 MiB of HBM per device.

```python
import math
import jax
import jax.numpy as jnp
from jax import lax

D = 4096
BLOCK = 128
STRETCH = 256
BLK_DEV = 16
BLOCKS = 64
COLUMNS = 8192
STRETCHES = 32


def draw_stretch_blocks(key, part):
    key = jax.random.fold_in(key, 7)
    owners = BLOCKS // BLK_DEV
    members = min(BLK_DEV, owners)
    layers = BLK_DEV // members
    stride = members // 2
    pairs = BLK_DEV // 2
    key_a, key_b, key_c = jax.random.split(key, 3)
    group_perm = jax.random.permutation(key_a, owners).astype(jnp.int32)
    rank_scores = jax.random.randint(key_b, (owners, BLK_DEV), 0, 4096, dtype=jnp.int32) * BLK_DEV
    rank_scores = rank_scores + jnp.arange(BLK_DEV, dtype=jnp.int32)[None, :]
    rank = jnp.argsort(jnp.argsort(rank_scores, axis=1), axis=1).reshape(BLOCKS).astype(jnp.int32)
    pair_scores = jax.random.randint(key_c, (owners, pairs), 0, 4096, dtype=jnp.int32) * pairs
    pair_scores = pair_scores + jnp.arange(pairs, dtype=jnp.int32)[None, :]
    pair_order = jnp.argsort(pair_scores, axis=1).astype(jnp.int32)
    block_ids = jnp.arange(BLOCKS, dtype=jnp.int32)
    owner_of = block_ids // BLK_DEV
    offset = rank % members
    layer = rank // members
    group = group_perm[(owner_of + offset) % owners]
    second = (offset >= stride).astype(jnp.int32)
    slot = offset % stride * layers + layer
    stretch = group * pairs + pair_order[group, slot]
    flat = jnp.zeros((BLOCKS,), jnp.int32).at[stretch * 2 + second].set(block_ids)
    return flat.reshape(BLOCKS // 2, 2)


def levels(key, extent, cuts, low, largest):
    def one(position, shards_of):
        steps = jax.random.uniform(jax.random.fold_in(jax.random.fold_in(key, 6), position), (shards_of,), jnp.float32, low / len(cuts), largest / len(cuts))
        return jnp.repeat(jnp.exp(steps), extent[position] // shards_of).reshape((-1,) + (1,) * (len(extent) - position - 1))

    factor_of = one(*cuts[0])
    for cut in cuts[1:]:
        factor_of = factor_of * one(*cut)
    return factor_of


def bell_draw(rng, shape, spread, limit, cuts=(), kind=jnp.bfloat16):
    factor_of = levels(rng, shape, cuts, -0.22, 0.18) if cuts else 1.0
    result = jax.random.normal(rng, shape, jnp.float32) * spread * factor_of
    return jnp.minimum(jnp.maximum(result, -limit), limit).astype(kind)


def setup_inputs(seed: int = 0, part: int = 0) -> dict:
    splits = jax.random.split(jax.random.key(seed), 4)
    part_splits = jax.random.split(jax.random.fold_in(splits[3], part), 4)
    return {
        "decoder": bell_draw(part_splits[0], (D, COLUMNS), D ** -0.5, 0.09375, ((0, 4), (1, 4))),
        "stretch_blocks": draw_stretch_blocks(jax.random.fold_in(jax.random.fold_in(splits[3], part), 71), part),
        "stretch_weight": jnp.clip(jnp.exp(jax.random.uniform(part_splits[2], (STRETCHES,), jnp.float32, math.log(24.0), math.log(192.0))), 24.0, 192.0),
    }


def reference(decoder, stretch_blocks, stretch_weight):
    blocks = decoder.reshape(D, BLOCKS, BLOCK)
    diagonal = jnp.eye(STRETCH, dtype=bool)

    def one_stretch(carried, inputs):
        block_ids, weight = inputs
        cols = jnp.take(blocks, block_ids.astype(jnp.int32), axis=1).reshape(D, STRETCH)
        gram = jnp.dot(cols.T, cols, preferred_element_type=jnp.float32)
        coefficient = (jnp.where(diagonal, jnp.float32(0.0), gram) * (4.0 * weight)).astype(jnp.bfloat16)
        grad = jnp.dot(cols, coefficient, preferred_element_type=jnp.float32).astype(jnp.bfloat16)
        grad_wide = grad.astype(jnp.float32)
        norm_cols = cols.astype(jnp.float32)
        along_dir = jnp.sum(norm_cols * grad_wide, axis=0)
        tangent = (grad_wide - along_dir[None, :] * norm_cols).astype(jnp.bfloat16)
        return carried, tangent.reshape(D, 2, BLOCK)

    _, pieces = lax.scan(one_stretch, jnp.int32(0), (stretch_blocks, stretch_weight))
    ordered = jnp.transpose(pieces, (1, 0, 2, 3)).reshape(D, BLOCKS, BLOCK)
    inverse = jnp.argsort(stretch_blocks.reshape(-1)).astype(jnp.int32)
    return jnp.take(ordered, inverse, axis=1).reshape(D, BLOCKS * BLOCK)
```

```python
import functools

import jax
import jax.numpy as jnp
from jax import lax
from jax.experimental import pallas as pl
from jax.experimental.pallas import tpu as pltpu
from jax.sharding import PartitionSpec as P

BLOCK = 128
STRETCH = 256
CHUNKS = (2, 2, 2, 1, 1)
LAG = 2

ANY = pl.BlockSpec(memory_space=pl.ANY)
VMEM = pl.BlockSpec(memory_space=pltpu.VMEM)
SMEM = pl.BlockSpec(memory_space=pltpu.SMEM)


def column(ref, block):
    start = block * BLOCK
    if not isinstance(block, int):
        start = pl.multiple_of(start, BLOCK)
    return ref.at[:, pl.ds(start, BLOCK)]


def plan(per_dev, blocks_ref, weight_ref, place_ref, scale_ref):
    me = lax.axis_index("outer")

    def one(c, counts):
        first, second = blocks_ref[c, 0], blocks_ref[c, 1]
        firsts, seconds = counts
        place_ref[0, firsts] = lax.rem(first, per_dev)
        scale_ref[0, firsts] = 4.0 * weight_ref[c]
        place_ref[1, seconds] = lax.rem(second, per_dev)
        firsts += (lax.div(first, per_dev) == me).astype(jnp.int32)
        seconds += (lax.div(second, per_dev) == me).astype(jnp.int32)
        return firsts, seconds

    lax.fori_loop(0, blocks_ref.shape[0], one, (jnp.int32(0), jnp.int32(0)))


def opening_kernel(per_dev, starts, sizes, blocks_ref, weight_ref, decoder_ref, place_ref, scale_ref, *rest):
    outs, sem = rest[:-1], rest[-1]
    plan(per_dev, blocks_ref, weight_ref, place_ref, scale_ref)
    copies = []
    for start, size, out in zip(starts, sizes, outs):
        for j in range(size):
            copies.append(
                pltpu.make_async_copy(
                    column(decoder_ref, place_ref[1, start + j]), column(out, j), sem.at[len(copies)]
                )
            )
            copies[-1].start()
    for copy in copies:
        copy.wait()


def gram_parts(x):
    gram = lax.dot_general(x, x, (((0,), (0,)), ((), ())), preferred_element_type=jnp.float32)
    row = lax.broadcasted_iota(jnp.int32, (BLOCK, BLOCK), 0)
    col = lax.broadcasted_iota(jnp.int32, (BLOCK, BLOCK), 1)
    own = jnp.where(row < col, gram[:BLOCK, :BLOCK], gram[BLOCK:, BLOCK:])
    return own, gram[:BLOCK, BLOCK:]


def tangents(x, own, cross, scale):
    row = lax.broadcasted_iota(jnp.int32, (BLOCK, BLOCK), 0)
    col = lax.broadcasted_iota(jnp.int32, (BLOCK, BLOCK), 1)
    upper = jnp.where(row < col, own, 0.0)
    lower = jnp.where(row > col, own, 0.0)
    gram = jnp.concatenate(
        [
            jnp.concatenate([upper + upper.T, cross], axis=1),
            jnp.concatenate([cross.T, lower + lower.T], axis=1),
        ],
        axis=0,
    )
    coef = (gram * scale).astype(jnp.bfloat16)
    along = jnp.sum(gram * coef.astype(jnp.float32), axis=0, keepdims=True)
    grad = jnp.dot(x, coef, preferred_element_type=jnp.float32).astype(jnp.bfloat16)
    return (grad.astype(jnp.float32) - along * x.astype(jnp.float32)).astype(jnp.bfloat16)


def step_kernel(spec, *refs):
    refs = list(refs)
    take = lambda: refs.pop(0)
    place_ref, scale_ref, decoder_ref = take(), take(), take()
    gram_in = take() if spec["gram"] else None
    final_in = take() if spec["final"] else None
    parts = [take() for _ in range(spec["ranks"])] if spec["final"] else None
    back_in = take() if spec["back"] else None
    if spec["aliased"]:
        take()
    gram_out = take() if spec["gram"] else None
    send_out = take() if spec["final"] or spec["pack"] else None
    out_ref = take() if spec["final"] or spec["back"] else None
    gram_x, final_x, final_t, load_sem, move_sem, store_sem = refs

    loads = {}

    def load(kind, scratch, source, start, size):
        for j in range(size):
            pair = (
                pltpu.make_async_copy(
                    column(decoder_ref, place_ref[0, start + j]),
                    scratch.at[j, :, pl.ds(0, BLOCK)],
                    load_sem.at[len(loads), 0],
                ),
                pltpu.make_async_copy(
                    column(source, j), scratch.at[j, :, pl.ds(BLOCK, BLOCK)], load_sem.at[len(loads), 1]
                ),
            )
            for copy in pair:
                copy.start()
            loads[kind, j] = pair

    moves = []

    def move(source, target):
        moves.append(pltpu.make_async_copy(source, target, move_sem.at[len(moves)]))
        moves[-1].start()

    if spec["pack"]:
        start, size = spec["pack"]
        for j in range(size):
            move(column(decoder_ref, place_ref[1, start + j]), column(send_out, j))
    if spec["gram"]:
        load("gram", gram_x, gram_in, *spec["gram"])
    if spec["final"]:
        load("final", final_x, final_in, *spec["final"])
    if spec["back"]:
        start, size = spec["back"]
        for j in range(size):
            move(column(back_in, j), column(out_ref, place_ref[1, start + j]))

    if spec["gram"]:
        for j in range(spec["gram"][1]):
            for copy in loads["gram", j]:
                copy.wait()
            gram_out[j, 0], gram_out[j, 1] = gram_parts(gram_x[j])

    stores = []
    if spec["final"]:
        start, size = spec["final"]
        for j in range(size):
            for copy in loads["final", j]:
                copy.wait()
            a, b, c, d = (part[j] for part in parts)
            total = (a + b) + (c + d)
            final_t[j] = tangents(final_x[j], total[0], total[1], scale_ref[0, start + j])
            for target, half in ((column(out_ref, place_ref[0, start + j]), 0), (column(send_out, j), 1)):
                stores.append(
                    pltpu.make_async_copy(
                        final_t.at[j, :, pl.ds(half * BLOCK, BLOCK)], target, store_sem.at[len(stores)]
                    )
                )
                stores[-1].start()
    for copy in moves + stores:
        copy.wait()


def shards(decoder, stretch_blocks, stretch_weight):
    width, columns = decoder.shape
    per_dev = columns // BLOCK
    half = per_dev // 2
    owners, ranks = lax.axis_size("outer"), lax.axis_size("inner")
    stride = min(owners, per_dev) // 2
    sizes = CHUNKS
    count = len(sizes)
    starts = [sum(sizes[:k]) for k in range(count)]
    chunk = lambda k: (starts[k], sizes[k])
    array = lambda k: jax.ShapeDtypeStruct((width, sizes[k] * BLOCK), decoder.dtype)
    out_shape = jax.ShapeDtypeStruct(decoder.shape, decoder.dtype)
    to_first = [(o, (o + stride) % owners) for o in range(owners)]
    to_second = [(o, (o - stride) % owners) for o in range(owners)]

    place, scale, *raw = pl.pallas_call(
        functools.partial(opening_kernel, per_dev, starts[:LAG], sizes[:LAG]),
        out_shape=[
            jax.ShapeDtypeStruct((2, half + 1), jnp.int32),
            jax.ShapeDtypeStruct((1, half + 1), jnp.float32),
        ]
        + [array(k) for k in range(LAG)],
        in_specs=[SMEM, SMEM, ANY],
        out_specs=[SMEM, SMEM] + [ANY] * LAG,
        scratch_shapes=[pltpu.SemaphoreType.DMA((per_dev,))],
        name="opening",
    )(stretch_blocks, stretch_weight, decoder)

    sends = [lax.ppermute(part, "outer", to_first) for part in raw]
    parts = {}
    out = None
    for step in range(2 * count):
        arrived = sends[step]
        gram = chunk(step) if step < count else None
        pack = chunk(step + LAG) if step + LAG < count else None
        turn = step + LAG - count
        final = chunk(turn) if 0 <= turn < count else None
        back = chunk(step - count) if step >= count else None
        spec = {"gram": gram, "pack": pack, "final": final, "back": back, "ranks": ranks, "aliased": out is not None}
        args, specs = [place, scale, decoder], [SMEM, SMEM, ANY]
        shapes, out_specs, aliases = [], [], {}
        if gram:
            args, specs = args + [arrived], specs + [ANY]
            shapes.append(jax.ShapeDtypeStruct((gram[1], 2, BLOCK, BLOCK), jnp.float32))
            out_specs.append(VMEM)
        if final:
            args, specs = args + [sends[turn]] + parts.pop(turn), specs + [ANY] + [VMEM] * ranks
        if back:
            args, specs = args + [arrived], specs + [ANY]
        if final or pack:
            shapes.append(array(turn if final else step + LAG))
            out_specs.append(ANY)
        if final or back:
            if out is not None:
                aliases = {len(args): len(shapes)}
                args, specs = args + [out], specs + [ANY]
            shapes.append(out_shape)
            out_specs.append(ANY)
        slot = max(sizes)
        results = list(
            pl.pallas_call(
                functools.partial(step_kernel, spec),
                out_shape=shapes,
                in_specs=specs,
                out_specs=out_specs,
                input_output_aliases=aliases,
                scratch_shapes=[
                    pltpu.VMEM((slot, width, STRETCH), decoder.dtype),
                    pltpu.VMEM((slot, width, STRETCH), decoder.dtype),
                    pltpu.VMEM((slot, width, STRETCH), decoder.dtype),
                    pltpu.SemaphoreType.DMA((2 * slot, 2)),
                    pltpu.SemaphoreType.DMA((2 * slot,)),
                    pltpu.SemaphoreType.DMA((2 * slot,)),
                ],
                compiler_params=pltpu.CompilerParams(vmem_limit_bytes=32 * 2**20),
                name="step",
            )(*args)
        )
        if gram:
            mine = results.pop(0)
            parts[step] = [mine] + [
                lax.ppermute(mine, "inner", [(i, i ^ hop) for i in range(ranks)]) for hop in range(1, ranks)
            ]
        if final or pack:
            sends.append(lax.ppermute(results.pop(0), "outer", to_second if final else to_first))
        if final or back:
            out = results.pop(0)
    return out


def solution(mesh):
    placed = (P("inner", ("groups", "outer")), P("groups", None), P("groups"))
    return jax.shard_map(
        shards,
        mesh=mesh,
        in_specs=placed,
        out_specs=P("inner", ("groups", "outer")),
        check_vma=False,
    )
```

```python
import functools

import jax
import jax.numpy as jnp
from jax import lax
from jax.experimental import pallas as pl
from jax.experimental.pallas import tpu as pltpu
from jax.sharding import PartitionSpec as P

BLOCK = 128
STRETCH = 256
CHUNKS = (1,2,2,2,1,)
LAG = 3

ANY = pl.BlockSpec(memory_space=pl.ANY)
HBM = pl.BlockSpec(memory_space=pltpu.HBM)
VMEM = pl.BlockSpec(memory_space=pltpu.VMEM)
SMEM = pl.BlockSpec(memory_space=pltpu.SMEM)


def column(ref, block):
    start = block * BLOCK
    if not isinstance(block, int):
        start = pl.multiple_of(start, BLOCK)
    return ref.at[:, pl.ds(start, BLOCK)]


def plan(per_dev, blocks_ref, weight_ref, place_ref, scale_ref):
    me = lax.axis_index("outer")

    def one(c, counts):
        first, second = blocks_ref[0, c], blocks_ref[1, c]
        firsts, seconds = counts
        place_ref[0, firsts] = lax.rem(first, per_dev)
        scale_ref[0, firsts] = 4.0 * weight_ref[c]
        place_ref[1, seconds] = lax.rem(second, per_dev)
        firsts += (lax.div(first, per_dev) == me).astype(jnp.int32)
        seconds += (lax.div(second, per_dev) == me).astype(jnp.int32)
        return firsts, seconds

    lax.fori_loop(0, blocks_ref.shape[1], one, (jnp.int32(0), jnp.int32(0)))


def opening_kernel(per_dev, starts, sizes, blocks_ref, weight_ref, decoder_ref, place_ref, scale_ref, *rest):
    outs, sem = rest[:-1], rest[-1]
    plan(per_dev, blocks_ref, weight_ref, place_ref, scale_ref)
    copies = []
    for start, size, out in zip(starts, sizes, outs):
        for j in range(size):
            copies.append(
                pltpu.make_async_copy(
                    column(decoder_ref, place_ref[1, start + j]), column(out, j), sem.at[len(copies)]
                )
            )
            copies[-1].start()
    for copy in copies:
        copy.wait()


def gram_parts(x):
    gram = lax.dot_general(x, x, (((0,), (0,)), ((), ())), preferred_element_type=jnp.float32)
    row = lax.broadcasted_iota(jnp.int32, (BLOCK, BLOCK), 0)
    col = lax.broadcasted_iota(jnp.int32, (BLOCK, BLOCK), 1)
    own = jnp.where(row < col, gram[:BLOCK, :BLOCK], gram[BLOCK:, BLOCK:])
    return own, gram[:BLOCK, BLOCK:]


def tangents(x, own, cross, scale):
    row = lax.broadcasted_iota(jnp.int32, (BLOCK, BLOCK), 0)
    col = lax.broadcasted_iota(jnp.int32, (BLOCK, BLOCK), 1)
    upper = jnp.where(row < col, own, 0.0)
    lower = jnp.where(row > col, own, 0.0)
    gram = jnp.concatenate(
        [
            jnp.concatenate([upper + upper.T, cross], axis=1),
            jnp.concatenate([cross.T, lower + lower.T], axis=1),
        ],
        axis=0,
    )
    coef = (gram * scale).astype(jnp.bfloat16)
    along = jnp.sum(gram * coef.astype(jnp.float32), axis=0, keepdims=True)
    grad = jnp.dot(x, coef, preferred_element_type=jnp.float32).astype(jnp.bfloat16)
    return (grad.astype(jnp.float32) - along * x.astype(jnp.float32)).astype(jnp.bfloat16)


def step_kernel(spec, *refs):
    refs = list(refs)
    take = lambda: refs.pop(0)
    place_ref, scale_ref, decoder_ref = take(), take(), take()
    gram_in = take() if spec["gram"] else None
    final_in = take() if spec["final"] else None
    parts = [take() for _ in range(spec["ranks"])] if spec["final"] else None
    back_in = take() if spec["back"] else None
    for _ in range(spec["unread"]):
        take()
    gram_out = take() if spec["gram"] else None
    send_out = take() if spec["final"] or spec["pack"] else None
    out_ref = take() if spec["final"] or spec["back"] else None
    gram_x, final_x, final_t, load_sem, move_sem, store_sem = refs

    loads = {}

    def load(kind, scratch, source, start, size):
        for j in range(size):
            pair = (
                pltpu.make_async_copy(
                    column(decoder_ref, place_ref[0, start + j]),
                    scratch.at[j, :, pl.ds(0, BLOCK)],
                    load_sem.at[len(loads), 0],
                ),
                pltpu.make_async_copy(
                    column(source, j), scratch.at[j, :, pl.ds(BLOCK, BLOCK)], load_sem.at[len(loads), 1]
                ),
            )
            for copy in pair:
                copy.start()
            loads[kind, j] = pair

    moves = []

    def move(source, target):
        moves.append(pltpu.make_async_copy(source, target, move_sem.at[len(moves)]))
        moves[-1].start()

    if spec["pack"]:
        start, size = spec["pack"]
        for j in range(size):
            move(column(decoder_ref, place_ref[1, start + j]), column(send_out, j))
    if spec["gram"]:
        load("gram", gram_x, gram_in, *spec["gram"])
    if spec["final"]:
        load("final", final_x, final_in, *spec["final"])
    if spec["back"]:
        start, size = spec["back"]
        for j in range(size):
            move(column(back_in, j), column(out_ref, place_ref[1, start + j]))

    if spec["gram"]:
        for j in range(spec["gram"][1]):
            for copy in loads["gram", j]:
                copy.wait()
            gram_out[j, 0], gram_out[j, 1] = gram_parts(gram_x[j])

    stores = []
    if spec["final"]:
        start, size = spec["final"]
        for j in range(size):
            for copy in loads["final", j]:
                copy.wait()
            a, b, c, d = (part[j] for part in parts)
            total = (a + b) + (c + d)
            final_t[j] = tangents(final_x[j], total[0], total[1], scale_ref[0, start + j])
            for target, half in ((column(out_ref, place_ref[0, start + j]), 0), (column(send_out, j), 1)):
                stores.append(
                    pltpu.make_async_copy(
                        final_t.at[j, :, pl.ds(half * BLOCK, BLOCK)], target, store_sem.at[len(stores)]
                    )
                )
                stores[-1].start()
    for copy in moves + stores:
        copy.wait()


def shards(decoder, stretch_blocks, stretch_weight):
    width, columns = decoder.shape
    per_dev = columns // BLOCK
    half = per_dev // 2
    owners, ranks = lax.axis_size("outer"), lax.axis_size("inner")
    stride = min(owners, per_dev) // 2
    sizes = CHUNKS
    count = len(sizes)
    starts = [sum(sizes[:k]) for k in range(count)]
    chunk = lambda k: (starts[k], sizes[k])
    array = lambda k: jax.ShapeDtypeStruct((width, sizes[k] * BLOCK), decoder.dtype)
    out_shape = jax.ShapeDtypeStruct(decoder.shape, decoder.dtype)
    to_first = [(o, (o + stride) % owners) for o in range(owners)]
    to_second = [(o, (o - stride) % owners) for o in range(owners)]

    place, scale, *raw = pl.pallas_call(
        functools.partial(opening_kernel, per_dev, starts[:LAG], sizes[:LAG]),
        out_shape=[
            jax.ShapeDtypeStruct((2, half + 1), jnp.int32),
            jax.ShapeDtypeStruct((1, half + 1), jnp.float32),
        ]
        + [array(k) for k in range(LAG)],
        in_specs=[SMEM, SMEM, ANY],
        out_specs=[SMEM, SMEM] + [ANY] * LAG,
        scratch_shapes=[pltpu.SemaphoreType.DMA((per_dev,))],
        compiler_params=pltpu.CompilerParams(vmem_limit_bytes=8 * 2**20),
        name="opening",
    )(stretch_blocks.T, stretch_weight, decoder)

    sends = [lax.ppermute(part, "outer", to_first) for part in raw]
    parts = {}
    out = chain = None
    for step in range(2 * count):
        arrived = sends[step]
        gram = chunk(step) if step < count else None
        pack = chunk(step + LAG) if step + LAG < count else None
        turn = step + LAG - count
        final = chunk(turn) if 0 <= turn < count else None
        back = chunk(step - count) if step >= count else None
        spec = {"gram": gram, "pack": pack, "final": final, "back": back, "ranks": ranks, "unread": 0}
        args, specs = [place, scale, decoder], [SMEM, SMEM, HBM]
        shapes, out_specs, aliases = [], [], {}
        if gram:
            args, specs = args + [arrived], specs + [ANY]
            shapes.append(jax.ShapeDtypeStruct((gram[1], 2, BLOCK, BLOCK), jnp.float32))
            out_specs.append(VMEM)
        if final:
            args, specs = args + [sends[turn]] + parts.pop(turn), specs + [ANY] + [VMEM] * ranks
        if back:
            args, specs = args + [arrived], specs + [ANY]
        if final or pack:
            shapes.append(array(turn if final else step + LAG))
            out_specs.append(ANY)
        if final or back:
            if out is not None:
                aliases = {len(args): len(shapes)}
                args, specs, chain = args + [out], specs + [ANY], None
                spec["unread"] += 1
            shapes.append(out_shape)
            out_specs.append(ANY)
        if chain is not None:
            args, specs = args + [chain], specs + [ANY]
            spec["unread"] += 1
        slot = max(sizes)
        results = list(
            pl.pallas_call(
                functools.partial(step_kernel, spec),
                out_shape=shapes,
                in_specs=specs,
                out_specs=out_specs,
                input_output_aliases=aliases,
                scratch_shapes=[
                    pltpu.VMEM((slot, width, STRETCH), decoder.dtype),
                    pltpu.VMEM((slot, width, STRETCH), decoder.dtype),
                    pltpu.VMEM((slot, width, STRETCH), decoder.dtype),
                    pltpu.SemaphoreType.DMA((2 * slot, 2)),
                    pltpu.SemaphoreType.DMA((2 * slot,)),
                    pltpu.SemaphoreType.DMA((2 * slot,)),
                ],
                compiler_params=pltpu.CompilerParams(vmem_limit_bytes=32 * 2**20),
                name="step",
            )(*args)
        )
        if gram:
            chain = mine = results.pop(0)
            parts[step] = [mine] + [
                lax.ppermute(mine, "inner", [(i, i ^ hop) for i in range(ranks)]) for hop in range(1, ranks)
            ]
        if final or pack:
            sends.append(lax.ppermute(results.pop(0), "outer", to_second if final else to_first))
        if final or back:
            out = results.pop(0)
    return out


def solution(mesh):
    placed = (P("inner", ("groups", "outer")), P("groups", None), P("groups"))
    return jax.shard_map(
        shards,
        mesh=mesh,
        in_specs=placed,
        out_specs=P("inner", ("groups", "outer")),
        check_vma=False,
    )
```

```python
import functools

import jax
import jax.numpy as jnp
from jax import lax
from jax.experimental import pallas as pl
from jax.experimental.pallas import tpu as pltpu
from jax.sharding import PartitionSpec as P

BLOCK = 128
STRETCH = 256
CHUNKS = (2,2,2,2,)
LAG = 2

ANY = pl.BlockSpec(memory_space=pl.ANY)
HBM = pl.BlockSpec(memory_space=pltpu.HBM)
VMEM = pl.BlockSpec(memory_space=pltpu.VMEM)
SMEM = pl.BlockSpec(memory_space=pltpu.SMEM)


def column(ref, block):
    start = block * BLOCK
    if not isinstance(block, int):
        start = pl.multiple_of(start, BLOCK)
    return ref.at[:, pl.ds(start, BLOCK)]


def plan(per_dev, blocks_ref, weight_ref, place_ref, scale_ref):
    me = lax.axis_index("outer")

    def one(c, counts):
        first, second = blocks_ref[0, c], blocks_ref[1, c]
        firsts, seconds = counts
        place_ref[0, firsts] = lax.rem(first, per_dev)
        scale_ref[0, firsts] = 4.0 * weight_ref[c]
        place_ref[1, seconds] = lax.rem(second, per_dev)
        firsts += (lax.div(first, per_dev) == me).astype(jnp.int32)
        seconds += (lax.div(second, per_dev) == me).astype(jnp.int32)
        return firsts, seconds

    lax.fori_loop(0, blocks_ref.shape[1], one, (jnp.int32(0), jnp.int32(0)))


def gather(decoder_ref, blocks, outs, sizes, sem):
    copies = []
    for size, out in zip(sizes, outs):
        for j in range(size):
            copies.append(
                pltpu.make_async_copy(
                    column(decoder_ref, blocks[len(copies)]), column(out, j), sem.at[len(copies)]
                )
            )
            copies[-1].start()
    for copy in copies:
        copy.wait()


def opening_kernel(per_dev, sizes, blocks_ref, decoder_ref, out_ref, held_ref, sem):
    me = lax.axis_index("outer")
    fetch = pltpu.make_async_copy(blocks_ref, held_ref, sem.at[0])
    fetch.start()
    fetch.wait()
    blocks, c = [], jnp.int32(0)
    for _ in range(sizes[0]):
        c = lax.while_loop(lambda c: lax.div(held_ref[1, c], per_dev) != me, lambda c: c + 1, c)
        blocks.append(lax.rem(held_ref[1, c], per_dev))
        c += 1
    gather(decoder_ref, blocks, [out_ref], sizes, sem)


def planning_kernel(per_dev, start, sizes, blocks_ref, weight_ref, decoder_ref, first_ref, place_ref, scale_ref, *rest):
    outs, sem = rest[:-1], rest[-1]
    plan(per_dev, blocks_ref, weight_ref, place_ref, scale_ref)
    gather(decoder_ref, [place_ref[1, start + j] for j in range(sum(sizes))], outs, sizes, sem)


def gram_parts(x):
    gram = lax.dot_general(x, x, (((0,), (0,)), ((), ())), preferred_element_type=jnp.float32)
    row = lax.broadcasted_iota(jnp.int32, (BLOCK, BLOCK), 0)
    col = lax.broadcasted_iota(jnp.int32, (BLOCK, BLOCK), 1)
    own = jnp.where(row < col, gram[:BLOCK, :BLOCK], gram[BLOCK:, BLOCK:])
    return own, gram[:BLOCK, BLOCK:]


def tangents(x, own, cross, scale):
    row = lax.broadcasted_iota(jnp.int32, (BLOCK, BLOCK), 0)
    col = lax.broadcasted_iota(jnp.int32, (BLOCK, BLOCK), 1)
    upper = jnp.where(row < col, own, 0.0)
    lower = jnp.where(row > col, own, 0.0)
    gram = jnp.concatenate(
        [
            jnp.concatenate([upper + upper.T, cross], axis=1),
            jnp.concatenate([cross.T, lower + lower.T], axis=1),
        ],
        axis=0,
    )
    coef = (gram * scale).astype(jnp.bfloat16)
    along = jnp.sum(gram * coef.astype(jnp.float32), axis=0, keepdims=True)
    grad = jnp.dot(x, coef, preferred_element_type=jnp.float32).astype(jnp.bfloat16)
    return (grad.astype(jnp.float32) - along * x.astype(jnp.float32)).astype(jnp.bfloat16)


def step_kernel(spec, *refs):
    refs = list(refs)
    take = lambda: refs.pop(0)
    place_ref, scale_ref, decoder_ref = take(), take(), take()
    gram_in = take() if spec["gram"] else None
    final_in = take() if spec["final"] else None
    parts = [take() for _ in range(spec["ranks"])] if spec["final"] else None
    back_in = take() if spec["back"] else None
    for _ in range(spec["unread"]):
        take()
    gram_out = take() if spec["gram"] else None
    send_out = take() if spec["final"] or spec["pack"] else None
    out_ref = take() if spec["final"] or spec["back"] else None
    gram_x, final_x, final_t, load_sem, move_sem, store_sem = refs

    loads = {}

    def load(kind, scratch, source, start, size):
        for j in range(size):
            pair = (
                pltpu.make_async_copy(
                    column(decoder_ref, place_ref[0, start + j]),
                    scratch.at[j, :, pl.ds(0, BLOCK)],
                    load_sem.at[len(loads), 0],
                ),
                pltpu.make_async_copy(
                    column(source, j), scratch.at[j, :, pl.ds(BLOCK, BLOCK)], load_sem.at[len(loads), 1]
                ),
            )
            for copy in pair:
                copy.start()
            loads[kind, j] = pair

    moves = []

    def move(source, target):
        moves.append(pltpu.make_async_copy(source, target, move_sem.at[len(moves)]))
        moves[-1].start()

    if spec["pack"]:
        start, size = spec["pack"]
        for j in range(size):
            move(column(decoder_ref, place_ref[1, start + j]), column(send_out, j))
    if spec["gram"]:
        load("gram", gram_x, gram_in, *spec["gram"])
    if spec["final"]:
        load("final", final_x, final_in, *spec["final"])
    if spec["back"]:
        start, size = spec["back"]
        for j in range(size):
            move(column(back_in, j), column(out_ref, place_ref[1, start + j]))

    if spec["gram"]:
        for j in range(spec["gram"][1]):
            for copy in loads["gram", j]:
                copy.wait()
            gram_out[j, 0], gram_out[j, 1] = gram_parts(gram_x[j])

    stores = []
    if spec["final"]:
        start, size = spec["final"]
        for j in range(size):
            for copy in loads["final", j]:
                copy.wait()
            a, b, c, d = (part[j] for part in parts)
            total = (a + b) + (c + d)
            final_t[j] = tangents(final_x[j], total[0], total[1], scale_ref[0, start + j])
            for target, half in ((column(out_ref, place_ref[0, start + j]), 0), (column(send_out, j), 1)):
                stores.append(
                    pltpu.make_async_copy(
                        final_t.at[j, :, pl.ds(half * BLOCK, BLOCK)], target, store_sem.at[len(stores)]
                    )
                )
                stores[-1].start()
    for copy in moves + stores:
        copy.wait()


def shards(decoder, stretch_blocks, stretch_weight):
    width, columns = decoder.shape
    per_dev = columns // BLOCK
    half = per_dev // 2
    owners, ranks = lax.axis_size("outer"), lax.axis_size("inner")
    stride = min(owners, per_dev) // 2
    sizes = CHUNKS
    count = len(sizes)
    starts = [sum(sizes[:k]) for k in range(count)]
    chunk = lambda k: (starts[k], sizes[k])
    array = lambda k: jax.ShapeDtypeStruct((width, sizes[k] * BLOCK), decoder.dtype)
    out_shape = jax.ShapeDtypeStruct(decoder.shape, decoder.dtype)
    to_first = [(o, (o + stride) % owners) for o in range(owners)]
    to_second = [(o, (o - stride) % owners) for o in range(owners)]

    stay = lambda x: pltpu.with_memory_space_constraint(x, pltpu.HBM)
    pairs, decoder = stay(stretch_blocks.T), stay(decoder)
    first = pl.pallas_call(
        functools.partial(opening_kernel, per_dev, sizes[:1]),
        out_shape=array(0),
        in_specs=[HBM, HBM],
        out_specs=ANY,
        scratch_shapes=[pltpu.SMEM(pairs.shape, jnp.int32), pltpu.SemaphoreType.DMA((sizes[0],))],
        compiler_params=pltpu.CompilerParams(vmem_limit_bytes=8 * 2**20),
        name="opening",
    )(pairs, decoder)
    place, scale, *raw = pl.pallas_call(
        functools.partial(planning_kernel, per_dev, starts[1], sizes[1:LAG]),
        out_shape=[
            jax.ShapeDtypeStruct((2, half + 1), jnp.int32),
            jax.ShapeDtypeStruct((1, half + 1), jnp.float32),
        ]
        + [array(k) for k in range(1, LAG)],
        in_specs=[SMEM, SMEM, HBM, ANY],
        out_specs=[SMEM, SMEM] + [ANY] * (LAG - 1),
        scratch_shapes=[pltpu.SemaphoreType.DMA((per_dev,))],
        compiler_params=pltpu.CompilerParams(vmem_limit_bytes=8 * 2**20),
        name="planning",
    )(stretch_blocks.T, stretch_weight, decoder, first)

    sends = [lax.ppermute(part, "outer", to_first) for part in [first] + raw]
    parts = {}
    out = chain = None
    for step in range(2 * count):
        arrived = sends[step]
        gram = chunk(step) if step < count else None
        pack = chunk(step + LAG) if step + LAG < count else None
        turn = step + LAG - count
        final = chunk(turn) if 0 <= turn < count else None
        back = chunk(step - count) if step >= count else None
        spec = {"gram": gram, "pack": pack, "final": final, "back": back, "ranks": ranks, "unread": 0}
        args, specs = [place, scale, decoder], [SMEM, SMEM, HBM]
        shapes, out_specs, aliases = [], [], {}
        if gram:
            args, specs = args + [arrived], specs + [ANY]
            shapes.append(jax.ShapeDtypeStruct((gram[1], 2, BLOCK, BLOCK), jnp.float32))
            out_specs.append(VMEM)
        if final:
            args, specs = args + [sends[turn]] + parts.pop(turn), specs + [ANY] + [VMEM] * ranks
        if back:
            args, specs = args + [arrived], specs + [ANY]
        if final or pack:
            shapes.append(array(turn if final else step + LAG))
            out_specs.append(ANY)
        if final or back:
            if out is not None:
                aliases = {len(args): len(shapes)}
                args, specs, chain = args + [out], specs + [ANY], None
                spec["unread"] += 1
            shapes.append(out_shape)
            out_specs.append(ANY)
        if chain is not None:
            args, specs = args + [chain], specs + [ANY]
            spec["unread"] += 1
        slot = max(sizes)
        results = list(
            pl.pallas_call(
                functools.partial(step_kernel, spec),
                out_shape=shapes,
                in_specs=specs,
                out_specs=out_specs,
                input_output_aliases=aliases,
                scratch_shapes=[
                    pltpu.VMEM((slot, width, STRETCH), decoder.dtype),
                    pltpu.VMEM((slot, width, STRETCH), decoder.dtype),
                    pltpu.VMEM((slot, width, STRETCH), decoder.dtype),
                    pltpu.SemaphoreType.DMA((2 * slot, 2)),
                    pltpu.SemaphoreType.DMA((2 * slot,)),
                    pltpu.SemaphoreType.DMA((2 * slot,)),
                ],
                compiler_params=pltpu.CompilerParams(vmem_limit_bytes=32 * 2**20),
                name="step",
            )(*args)
        )
        if gram:
            chain = mine = results.pop(0)
            parts[step] = [mine] + [
                lax.ppermute(mine, "inner", [(i, i ^ hop) for i in range(ranks)]) for hop in range(1, ranks)
            ]
        if final or pack:
            sends.append(lax.ppermute(results.pop(0), "outer", to_second if final else to_first))
        if final or back:
            out = results.pop(0)
    return out


def solution(mesh):
    placed = (P("inner", ("groups", "outer")), P("groups", None), P("groups"))
    return jax.shard_map(
        shards,
        mesh=mesh,
        in_specs=placed,
        out_specs=P("inner", ("groups", "outer")),
        check_vma=False,
    )
```

```python
import functools

import jax
import jax.numpy as jnp
from jax import lax
from jax.experimental import pallas as pl
from jax.experimental.pallas import tpu as pltpu
from jax.sharding import PartitionSpec as P

BLOCK = 128
STRETCH = 256
CHUNKS = (2, 2, 2, 2)
LAG = 2

ANY = pl.BlockSpec(memory_space=pl.ANY)
HBM = pl.BlockSpec(memory_space=pltpu.HBM)
VMEM = pl.BlockSpec(memory_space=pltpu.VMEM)
SMEM = pl.BlockSpec(memory_space=pltpu.SMEM)


def column(ref, block):
    start = block * BLOCK
    if not isinstance(block, int):
        start = pl.multiple_of(start, BLOCK)
    return ref.at[:, pl.ds(start, BLOCK)]


def plan(per_dev, stride, blocks_ref, weight_ref, place_ref, scale_ref):
    me, owners = lax.axis_index("outer"), lax.axis_size("outer")
    half = per_dev // 2

    def mated(c, carry):
        first, second = blocks_ref[0, c], blocks_ref[1, c]
        first_mine = lax.div(first, per_dev) == me
        mine = jnp.where(first_mine, first, second)
        other = lax.rem(jnp.where(first_mine, second, first), per_dev)
        upper = me >= stride
        local = lax.rem(mine, per_dev)
        key = jnp.where(upper, local, other)
        spare = lax.div(mine, per_dev) != me
        keeps = (key >= half) == upper
        slot = lax.rem(key, half)
        kept = jnp.where(spare | jnp.logical_not(keeps), half, slot)
        place_ref[0, kept] = local
        scale_ref[0, kept] = 4.0 * weight_ref[c]
        place_ref[1, jnp.where(spare | keeps, half, slot)] = local
        return carry

    def one(c, counts):
        first, second = blocks_ref[0, c], blocks_ref[1, c]
        firsts, seconds = counts
        place_ref[0, firsts] = lax.rem(first, per_dev)
        scale_ref[0, firsts] = 4.0 * weight_ref[c]
        place_ref[1, seconds] = lax.rem(second, per_dev)
        firsts += (lax.div(first, per_dev) == me).astype(jnp.int32)
        seconds += (lax.div(second, per_dev) == me).astype(jnp.int32)
        return firsts, seconds

    if owners == 2 * stride:
        lax.fori_loop(0, blocks_ref.shape[1], mated, jnp.int32(0))
    else:
        lax.fori_loop(0, blocks_ref.shape[1], one, (jnp.int32(0), jnp.int32(0)))


def gather(decoder_ref, blocks, outs, sizes, sem):
    copies = []
    for size, out in zip(sizes, outs):
        for j in range(size):
            copies.append(
                pltpu.make_async_copy(
                    column(decoder_ref, blocks[len(copies)]), column(out, j), sem.at[len(copies)]
                )
            )
            copies[-1].start()
    for copy in copies:
        copy.wait()


def opening_kernel(per_dev, stride, sizes, blocks_ref, decoder_ref, out_ref, held_ref, sem):
    me, owners = lax.axis_index("outer"), lax.axis_size("outer")
    half = per_dev // 2

    def fetch():
        copy = pltpu.make_async_copy(blocks_ref, held_ref, sem.at[0])
        copy.start()
        copy.wait()

    if owners == 2 * stride:

        @pl.when(me >= stride)
        def _():
            gather(decoder_ref, range(sizes[0]), [out_ref], sizes, sem)

        @pl.when(me < stride)
        def _():
            fetch()
            blocks = []
            for j in range(sizes[0]):
                wanted = (me + stride) * per_dev + half + j
                c = lax.while_loop(
                    lambda c: (held_ref[0, c] != wanted) & (held_ref[1, c] != wanted), lambda c: c + 1, jnp.int32(0)
                )
                mate = jnp.where(held_ref[0, c] == wanted, held_ref[1, c], held_ref[0, c])
                blocks.append(lax.rem(mate, per_dev))
            gather(decoder_ref, blocks, [out_ref], sizes, sem)

    else:
        fetch()
        blocks, c = [], jnp.int32(0)
        for _ in range(sizes[0]):
            c = lax.while_loop(lambda c: lax.div(held_ref[1, c], per_dev) != me, lambda c: c + 1, c)
            blocks.append(lax.rem(held_ref[1, c], per_dev))
            c += 1
        gather(decoder_ref, blocks, [out_ref], sizes, sem)


def planning_kernel(per_dev, stride, start, sizes, blocks_ref, weight_ref, decoder_ref, first_ref, place_ref, scale_ref, *rest):
    outs, sem = rest[:-1], rest[-1]
    plan(per_dev, stride, blocks_ref, weight_ref, place_ref, scale_ref)
    gather(decoder_ref, [place_ref[1, start + j] for j in range(sum(sizes))], outs, sizes, sem)


def gram_parts(x):
    gram = lax.dot_general(x, x, (((0,), (0,)), ((), ())), preferred_element_type=jnp.float32)
    row = lax.broadcasted_iota(jnp.int32, (BLOCK, BLOCK), 0)
    col = lax.broadcasted_iota(jnp.int32, (BLOCK, BLOCK), 1)
    own = jnp.where(row < col, gram[:BLOCK, :BLOCK], gram[BLOCK:, BLOCK:])
    return own, gram[:BLOCK, BLOCK:]


def tangents(x, own, cross, scale):
    row = lax.broadcasted_iota(jnp.int32, (BLOCK, BLOCK), 0)
    col = lax.broadcasted_iota(jnp.int32, (BLOCK, BLOCK), 1)
    upper = jnp.where(row < col, own, 0.0)
    lower = jnp.where(row > col, own, 0.0)
    gram = jnp.concatenate(
        [
            jnp.concatenate([upper + upper.T, cross], axis=1),
            jnp.concatenate([cross.T, lower + lower.T], axis=1),
        ],
        axis=0,
    )
    coef = (gram * scale).astype(jnp.bfloat16)
    along = jnp.sum(gram * coef.astype(jnp.float32), axis=0, keepdims=True)
    grad = jnp.dot(x, coef, preferred_element_type=jnp.float32).astype(jnp.bfloat16)
    return (grad.astype(jnp.float32) - along * x.astype(jnp.float32)).astype(jnp.bfloat16)


def step_kernel(spec, *refs):
    refs = list(refs)
    take = lambda: refs.pop(0)
    place_ref = take()
    scale_ref, decoder_ref = (None, None) if spec["lean"] else (take(), take())
    gram_in = take() if spec["gram"] else None
    final_in = take() if spec["final"] else None
    parts = [take() for _ in range(spec["ranks"])] if spec["final"] else None
    back_in = take() if spec["back"] else None
    for _ in range(spec["unread"]):
        take()
    gram_out = take() if spec["gram"] else None
    send_outs = [take() for _ in range(spec["sends"])]
    out_ref = take() if spec["final"] or spec["back"] else None
    gram_x, final_x, final_t, load_sem, move_sem, store_sem = (None,) * 4 + (refs[0], None) if spec["lean"] else refs

    loads = {}

    def load(kind, scratch, source, start, size):
        for j in range(size):
            pair = (
                pltpu.make_async_copy(
                    column(decoder_ref, place_ref[0, start + j]),
                    scratch.at[j, :, pl.ds(0, BLOCK)],
                    load_sem.at[len(loads), 0],
                ),
                pltpu.make_async_copy(
                    column(source, j), scratch.at[j, :, pl.ds(BLOCK, BLOCK)], load_sem.at[len(loads), 1]
                ),
            )
            for copy in pair:
                copy.start()
            loads[kind, j] = pair

    moves = []

    def move(source, target):
        moves.append(pltpu.make_async_copy(source, target, move_sem.at[len(moves)]))
        moves[-1].start()

    if spec["pack"]:
        start, size = spec["pack"]
        for j in range(size):
            move(column(decoder_ref, place_ref[1, start + j]), column(send_outs[0], j))
    if spec["gram"]:
        load("gram", gram_x, gram_in, *spec["gram"])
    if spec["final"]:
        load("final", final_x, final_in, *spec["final"])
    if spec["back"]:
        start, size = spec["back"]
        for j in range(size):
            move(column(back_in, j), column(out_ref, place_ref[1, start + j]))

    if spec["gram"]:
        for j in range(spec["gram"][1]):
            for copy in loads["gram", j]:
                copy.wait()
            gram_out[j, 0], gram_out[j, 1] = gram_parts(gram_x[j])

    stores = []
    if spec["final"]:
        start, size = spec["final"]
        for j in range(size):
            for copy in loads["final", j]:
                copy.wait()
            a, b, c, d = (part[j] for part in parts)
            total = (a + b) + (c + d)
            final_t[j] = tangents(final_x[j], total[0], total[1], scale_ref[0, start + j])
            returned = column(send_outs[0], j) if len(send_outs) == 1 else send_outs[j]
            for target, half in ((column(out_ref, place_ref[0, start + j]), 0), (returned, 1)):
                stores.append(
                    pltpu.make_async_copy(
                        final_t.at[j, :, pl.ds(half * BLOCK, BLOCK)], target, store_sem.at[len(stores)]
                    )
                )
                stores[-1].start()
    for copy in moves + stores:
        copy.wait()


def shards(decoder, stretch_blocks, stretch_weight):
    width, columns = decoder.shape
    per_dev = columns // BLOCK
    half = per_dev // 2
    owners, ranks = lax.axis_size("outer"), lax.axis_size("inner")
    stride = min(owners, per_dev) // 2
    sizes = CHUNKS
    count = len(sizes)
    starts = [sum(sizes[:k]) for k in range(count)]
    chunk = lambda k: (starts[k], sizes[k])
    array = lambda k: jax.ShapeDtypeStruct((width, sizes[k] * BLOCK), decoder.dtype)
    out_shape = jax.ShapeDtypeStruct(decoder.shape, decoder.dtype)
    to_first = [(o, (o + stride) % owners) for o in range(owners)]
    to_second = [(o, (o - stride) % owners) for o in range(owners)]

    stay = lambda x: pltpu.with_memory_space_constraint(x, pltpu.HBM)
    pairs, decoder = stay(stretch_blocks.T), stay(decoder)
    first = pl.pallas_call(
        functools.partial(opening_kernel, per_dev, stride, sizes[:1]),
        out_shape=array(0),
        in_specs=[HBM, HBM],
        out_specs=ANY,
        scratch_shapes=[pltpu.SMEM(pairs.shape, jnp.int32), pltpu.SemaphoreType.DMA((sizes[0],))],
        compiler_params=pltpu.CompilerParams(vmem_limit_bytes=8 * 2**20),
        name="opening",
    )(pairs, decoder)
    place, scale, *raw = pl.pallas_call(
        functools.partial(planning_kernel, per_dev, stride, starts[1], sizes[1:LAG]),
        out_shape=[
            jax.ShapeDtypeStruct((2, half + 1), jnp.int32),
            jax.ShapeDtypeStruct((1, half + 1), jnp.float32),
        ]
        + [array(k) for k in range(1, LAG)],
        in_specs=[SMEM, SMEM, HBM, ANY],
        out_specs=[SMEM, SMEM] + [ANY] * (LAG - 1),
        scratch_shapes=[pltpu.SemaphoreType.DMA((per_dev,))],
        compiler_params=pltpu.CompilerParams(vmem_limit_bytes=8 * 2**20),
        name="planning",
    )(stretch_blocks.T, stretch_weight, decoder, first)

    sends = [lax.ppermute(part, "outer", to_first) for part in [first] + raw]
    parts = {}
    out = chain = None
    for step in range(2 * count - 1):
        arrived = sends[step]
        gram = chunk(step) if step < count else None
        pack = chunk(step + LAG) if step + LAG < count else None
        turn = step + LAG - count
        final = chunk(turn) if 0 <= turn < count else None
        back = chunk(step - count) if step >= count else None
        spec = {"gram": gram, "pack": pack, "final": final, "back": back, "ranks": ranks, "unread": 0}
        spec["lean"] = not (gram or pack or final)
        args, specs = [place], [SMEM]
        if not spec["lean"]:
            args, specs = args + [scale, decoder], specs + [SMEM, HBM]
        shapes, out_specs, aliases = [], [], {}
        if gram:
            args, specs = args + [arrived], specs + [ANY]
            shapes.append(jax.ShapeDtypeStruct((gram[1], 2, BLOCK, BLOCK), jnp.float32))
            out_specs.append(VMEM)
        if final:
            args, specs = args + [sends[turn]] + parts.pop(turn), specs + [ANY] + [VMEM] * ranks
        if back:
            args, specs = args + [arrived], specs + [ANY]
        spec["sends"] = int(bool(final or pack))
        if turn == count - 1:
            spec["sends"] = sizes[turn]
            shapes += [jax.ShapeDtypeStruct((width, BLOCK), decoder.dtype)] * sizes[turn]
            out_specs += [ANY] * sizes[turn]
        elif final or pack:
            shapes.append(array(turn if final else step + LAG))
            out_specs.append(ANY)
        if final or back:
            if out is not None:
                aliases = {len(args): len(shapes)}
                args, specs, chain = args + [out], specs + [ANY], None
                spec["unread"] += 1
            shapes.append(out_shape)
            out_specs.append(ANY)
        if chain is not None:
            args, specs = args + [chain], specs + [ANY]
            spec["unread"] += 1
        slot = max(sizes)
        results = list(
            pl.pallas_call(
                functools.partial(step_kernel, spec),
                out_shape=shapes,
                in_specs=specs,
                out_specs=out_specs,
                input_output_aliases=aliases,
                scratch_shapes=[pltpu.SemaphoreType.DMA((2 * slot,))]
                if spec["lean"]
                else [
                    pltpu.VMEM((slot, width, STRETCH), decoder.dtype),
                    pltpu.VMEM((slot, width, STRETCH), decoder.dtype),
                    pltpu.VMEM((slot, width, STRETCH), decoder.dtype),
                    pltpu.SemaphoreType.DMA((2 * slot, 2)),
                    pltpu.SemaphoreType.DMA((2 * slot,)),
                    pltpu.SemaphoreType.DMA((2 * slot,)),
                ],
                compiler_params=pltpu.CompilerParams(vmem_limit_bytes=32 * 2**20),
                name="step",
            )(*args)
        )
        if gram:
            chain = mine = results.pop(0)
            parts[step] = [mine] + [
                lax.ppermute(mine, "inner", [(i, i ^ hop) for i in range(ranks)]) for hop in range(1, ranks)
            ]
        for _ in range(spec["sends"]):
            sends.append(lax.ppermute(results.pop(0), "outer", to_second if final else to_first))
        if final or back:
            out = results.pop(0)
    for j in range(sizes[-1]):
        out = lax.dynamic_update_slice(out, sends[j - sizes[-1]], (0, place[1, half - sizes[-1] + j] * BLOCK))
    return out


def solution(mesh):
    placed = (P("inner", ("groups", "outer")), P("groups", None), P("groups"))
    return jax.shard_map(
        shards,
        mesh=mesh,
        in_specs=placed,
        out_specs=P("inner", ("groups", "outer")),
        check_vma=False,
    )
```

```python
import functools

import jax
import jax.numpy as jnp
from jax import lax
from jax.experimental import pallas as pl
from jax.experimental.pallas import tpu as pltpu
from jax.sharding import PartitionSpec as P

BLOCK = 128
STRETCH = 256
CHUNKS = (2, 2, 2, 2)
LAG = 2

ANY = pl.BlockSpec(memory_space=pl.ANY)
HBM = pl.BlockSpec(memory_space=pltpu.HBM)
VMEM = pl.BlockSpec(memory_space=pltpu.VMEM)
SMEM = pl.BlockSpec(memory_space=pltpu.SMEM)


def column(ref, block):
    start = block * BLOCK
    if not isinstance(block, int):
        start = pl.multiple_of(start, BLOCK)
    return ref.at[:, pl.ds(start, BLOCK)]


def plan(per_dev, stride, blocks_ref, weight_ref, place_ref, scale_ref):
    me, owners = lax.axis_index("outer"), lax.axis_size("outer")
    half = per_dev // 2

    def mated(c, carry):
        first, second = blocks_ref[0, c], blocks_ref[1, c]
        first_mine = lax.div(first, per_dev) == me
        mine = jnp.where(first_mine, first, second)
        other = lax.rem(jnp.where(first_mine, second, first), per_dev)
        upper = me >= stride
        local = lax.rem(mine, per_dev)
        key = jnp.where(upper, local, other)
        spare = lax.div(mine, per_dev) != me
        keeps = (key >= half) == upper
        slot = lax.rem(key, half)
        kept = jnp.where(spare | jnp.logical_not(keeps), half, slot)
        place_ref[0, kept] = local
        scale_ref[0, kept] = 4.0 * weight_ref[c]
        place_ref[1, jnp.where(spare | keeps, half, slot)] = local
        return carry

    def one(c, counts):
        first, second = blocks_ref[0, c], blocks_ref[1, c]
        firsts, seconds = counts
        place_ref[0, firsts] = lax.rem(first, per_dev)
        scale_ref[0, firsts] = 4.0 * weight_ref[c]
        place_ref[1, seconds] = lax.rem(second, per_dev)
        firsts += (lax.div(first, per_dev) == me).astype(jnp.int32)
        seconds += (lax.div(second, per_dev) == me).astype(jnp.int32)
        return firsts, seconds

    if owners == 2 * stride:
        lax.fori_loop(0, blocks_ref.shape[1], mated, jnp.int32(0))
    else:
        lax.fori_loop(0, blocks_ref.shape[1], one, (jnp.int32(0), jnp.int32(0)))


def gather(decoder_ref, blocks, outs, sizes, sem):
    copies = []
    for size, out in zip(sizes, outs):
        for j in range(size):
            copies.append(
                pltpu.make_async_copy(
                    column(decoder_ref, blocks[len(copies)]), column(out, j), sem.at[len(copies)]
                )
            )
            copies[-1].start()
    for copy in copies:
        copy.wait()


def opening_kernel(per_dev, stride, sizes, blocks_ref, decoder_ref, out_ref, held_ref, sem):
    me, owners = lax.axis_index("outer"), lax.axis_size("outer")
    half = per_dev // 2

    def fetch():
        copy = pltpu.make_async_copy(blocks_ref, held_ref, sem.at[0])
        copy.start()
        copy.wait()

    if owners == 2 * stride:

        @pl.when(me >= stride)
        def _():
            gather(decoder_ref, range(sizes[0]), [out_ref], sizes, sem)

        @pl.when(me < stride)
        def _():
            fetch()
            copies = []
            for j in range(sizes[0]):
                wanted = (me + stride) * per_dev + half + j
                mate = jnp.int32(0)
                for c in range(held_ref.shape[1]):
                    first, second = held_ref[0, c], held_ref[1, c]
                    mate = jnp.where(first == wanted, second, jnp.where(second == wanted, first, mate))
                copies.append(
                    pltpu.make_async_copy(column(decoder_ref, lax.rem(mate, per_dev)), column(out_ref, j), sem.at[j])
                )
                copies[-1].start()
            for copy in copies:
                copy.wait()

    else:
        fetch()
        blocks, c = [], jnp.int32(0)
        for _ in range(sizes[0]):
            c = lax.while_loop(lambda c: lax.div(held_ref[1, c], per_dev) != me, lambda c: c + 1, c)
            blocks.append(lax.rem(held_ref[1, c], per_dev))
            c += 1
        gather(decoder_ref, blocks, [out_ref], sizes, sem)


def planning_kernel(per_dev, stride, start, sizes, blocks_ref, weight_ref, decoder_ref, first_ref, place_ref, scale_ref, *rest):
    outs, sem = rest[:-1], rest[-1]
    plan(per_dev, stride, blocks_ref, weight_ref, place_ref, scale_ref)
    gather(decoder_ref, [place_ref[1, start + j] for j in range(sum(sizes))], outs, sizes, sem)


def gram_parts(x):
    gram = lax.dot_general(x, x, (((0,), (0,)), ((), ())), preferred_element_type=jnp.float32)
    row = lax.broadcasted_iota(jnp.int32, (BLOCK, BLOCK), 0)
    col = lax.broadcasted_iota(jnp.int32, (BLOCK, BLOCK), 1)
    own = jnp.where(row < col, gram[:BLOCK, :BLOCK], gram[BLOCK:, BLOCK:])
    return own, gram[:BLOCK, BLOCK:]


def tangents(x, own, cross, scale):
    row = lax.broadcasted_iota(jnp.int32, (BLOCK, BLOCK), 0)
    col = lax.broadcasted_iota(jnp.int32, (BLOCK, BLOCK), 1)
    upper = jnp.where(row < col, own, 0.0)
    lower = jnp.where(row > col, own, 0.0)
    gram = jnp.concatenate(
        [
            jnp.concatenate([upper + upper.T, cross], axis=1),
            jnp.concatenate([cross.T, lower + lower.T], axis=1),
        ],
        axis=0,
    )
    coef = (gram * scale).astype(jnp.bfloat16)
    along = jnp.sum(gram * coef.astype(jnp.float32), axis=0, keepdims=True)
    grad = jnp.dot(x, coef, preferred_element_type=jnp.float32).astype(jnp.bfloat16)
    return (grad.astype(jnp.float32) - along * x.astype(jnp.float32)).astype(jnp.bfloat16)


def step_kernel(spec, *refs):
    refs = list(refs)
    take = lambda: refs.pop(0)
    place_ref = take()
    scale_ref, decoder_ref = (None, None) if spec["lean"] else (take(), take())
    gram_in = take() if spec["gram"] else None
    final_in = take() if spec["final"] else None
    parts = [take() for _ in range(spec["ranks"])] if spec["final"] else None
    back_in = take() if spec["back"] else None
    for _ in range(spec["unread"]):
        take()
    gram_out = take() if spec["gram"] else None
    send_outs = [take() for _ in range(spec["sends"])]
    out_ref = take() if spec["final"] or spec["back"] else None
    gram_x, final_x, final_t, load_sem, move_sem, store_sem = (None,) * 4 + (refs[0], None) if spec["lean"] else refs

    loads = {}

    def load(kind, scratch, source, start, size):
        for j in range(size):
            pair = (
                pltpu.make_async_copy(
                    column(decoder_ref, place_ref[0, start + j]),
                    scratch.at[j, :, pl.ds(0, BLOCK)],
                    load_sem.at[len(loads), 0],
                ),
                pltpu.make_async_copy(
                    column(source, j), scratch.at[j, :, pl.ds(BLOCK, BLOCK)], load_sem.at[len(loads), 1]
                ),
            )
            for copy in pair:
                copy.start()
            loads[kind, j] = pair

    moves = []

    def move(source, target):
        moves.append(pltpu.make_async_copy(source, target, move_sem.at[len(moves)]))
        moves[-1].start()

    if spec["pack"]:
        start, size = spec["pack"]
        for j in range(size):
            move(column(decoder_ref, place_ref[1, start + j]), column(send_outs[0], j))
    if spec["gram"]:
        load("gram", gram_x, gram_in, *spec["gram"])
    if spec["final"]:
        load("final", final_x, final_in, *spec["final"])
    if spec["back"]:
        start, size = spec["back"]
        for j in range(size):
            move(column(back_in, j), column(out_ref, place_ref[1, start + j]))

    if spec["gram"]:
        for j in range(spec["gram"][1]):
            for copy in loads["gram", j]:
                copy.wait()
            gram_out[j, 0], gram_out[j, 1] = gram_parts(gram_x[j])

    stores = []
    if spec["final"]:
        start, size = spec["final"]
        for j in range(size):
            for copy in loads["final", j]:
                copy.wait()
            a, b, c, d = (part[j] for part in parts)
            total = (a + b) + (c + d)
            final_t[j] = tangents(final_x[j], total[0], total[1], scale_ref[0, start + j])
            returned = column(send_outs[0], j) if len(send_outs) == 1 else send_outs[j]
            for target, half in ((column(out_ref, place_ref[0, start + j]), 0), (returned, 1)):
                stores.append(
                    pltpu.make_async_copy(
                        final_t.at[j, :, pl.ds(half * BLOCK, BLOCK)], target, store_sem.at[len(stores)]
                    )
                )
                stores[-1].start()
    for copy in moves + stores:
        copy.wait()


def shards(decoder, stretch_blocks, stretch_weight):
    width, columns = decoder.shape
    per_dev = columns // BLOCK
    half = per_dev // 2
    owners, ranks = lax.axis_size("outer"), lax.axis_size("inner")
    stride = min(owners, per_dev) // 2
    sizes = CHUNKS
    count = len(sizes)
    starts = [sum(sizes[:k]) for k in range(count)]
    chunk = lambda k: (starts[k], sizes[k])
    array = lambda k: jax.ShapeDtypeStruct((width, sizes[k] * BLOCK), decoder.dtype)
    out_shape = jax.ShapeDtypeStruct(decoder.shape, decoder.dtype)
    to_first = [(o, (o + stride) % owners) for o in range(owners)]
    to_second = [(o, (o - stride) % owners) for o in range(owners)]

    stay = lambda x: pltpu.with_memory_space_constraint(x, pltpu.HBM)
    pairs, decoder = stay(stretch_blocks.T), stay(decoder)
    first = pl.pallas_call(
        functools.partial(opening_kernel, per_dev, stride, sizes[:1]),
        out_shape=array(0),
        in_specs=[HBM, HBM],
        out_specs=ANY,
        scratch_shapes=[pltpu.SMEM(pairs.shape, jnp.int32), pltpu.SemaphoreType.DMA((sizes[0],))],
        compiler_params=pltpu.CompilerParams(vmem_limit_bytes=8 * 2**20),
        name="opening",
    )(pairs, decoder)
    place, scale, *raw = pl.pallas_call(
        functools.partial(planning_kernel, per_dev, stride, starts[1], sizes[1:LAG]),
        out_shape=[
            jax.ShapeDtypeStruct((2, half + 1), jnp.int32),
            jax.ShapeDtypeStruct((1, half + 1), jnp.float32),
        ]
        + [array(k) for k in range(1, LAG)],
        in_specs=[SMEM, SMEM, HBM, ANY],
        out_specs=[SMEM, SMEM] + [ANY] * (LAG - 1),
        scratch_shapes=[pltpu.SemaphoreType.DMA((per_dev,))],
        compiler_params=pltpu.CompilerParams(vmem_limit_bytes=8 * 2**20),
        name="planning",
    )(stretch_blocks.T, stretch_weight, decoder, first)

    sends = [lax.ppermute(part, "outer", to_first) for part in [first] + raw]
    parts = {}
    out = chain = None
    for step in range(2 * count - 1):
        arrived = sends[step]
        gram = chunk(step) if step < count else None
        pack = chunk(step + LAG) if step + LAG < count else None
        turn = step + LAG - count
        final = chunk(turn) if 0 <= turn < count else None
        back = chunk(step - count) if step >= count else None
        spec = {"gram": gram, "pack": pack, "final": final, "back": back, "ranks": ranks, "unread": 0}
        spec["lean"] = not (gram or pack or final)
        args, specs = [place], [SMEM]
        if not spec["lean"]:
            args, specs = args + [scale, decoder], specs + [SMEM, HBM]
        shapes, out_specs, aliases = [], [], {}
        if gram:
            args, specs = args + [arrived], specs + [ANY]
            shapes.append(jax.ShapeDtypeStruct((gram[1], 2, BLOCK, BLOCK), jnp.float32))
            out_specs.append(VMEM)
        if final:
            args, specs = args + [sends[turn]] + parts.pop(turn), specs + [ANY] + [VMEM] * ranks
        if back:
            args, specs = args + [arrived], specs + [ANY]
        spec["sends"] = int(bool(final or pack))
        if turn == count - 1:
            spec["sends"] = sizes[turn]
            shapes += [jax.ShapeDtypeStruct((width, BLOCK), decoder.dtype)] * sizes[turn]
            out_specs += [ANY] * sizes[turn]
        elif final or pack:
            shapes.append(array(turn if final else step + LAG))
            out_specs.append(ANY)
        if final or back:
            if out is not None:
                aliases = {len(args): len(shapes)}
                args, specs, chain = args + [out], specs + [ANY], None
                spec["unread"] += 1
            shapes.append(out_shape)
            out_specs.append(ANY)
        if chain is not None:
            args, specs = args + [chain], specs + [ANY]
            spec["unread"] += 1
        slot = max(sizes)
        results = list(
            pl.pallas_call(
                functools.partial(step_kernel, spec),
                out_shape=shapes,
                in_specs=specs,
                out_specs=out_specs,
                input_output_aliases=aliases,
                scratch_shapes=[pltpu.SemaphoreType.DMA((2 * slot,))]
                if spec["lean"]
                else [
                    pltpu.VMEM((slot, width, STRETCH), decoder.dtype),
                    pltpu.VMEM((slot, width, STRETCH), decoder.dtype),
                    pltpu.VMEM((slot, width, STRETCH), decoder.dtype),
                    pltpu.SemaphoreType.DMA((2 * slot, 2)),
                    pltpu.SemaphoreType.DMA((2 * slot,)),
                    pltpu.SemaphoreType.DMA((2 * slot,)),
                ],
                compiler_params=pltpu.CompilerParams(vmem_limit_bytes=32 * 2**20),
                name="step",
            )(*args)
        )
        if gram:
            chain = mine = results.pop(0)
            parts[step] = [mine] + [
                lax.ppermute(mine, "inner", [(i, i ^ hop) for i in range(ranks)]) for hop in range(1, ranks)
            ]
        for _ in range(spec["sends"]):
            sends.append(lax.ppermute(results.pop(0), "outer", to_second if final else to_first))
        if final or back:
            out = results.pop(0)
    for j in range(sizes[-1]):
        out = lax.dynamic_update_slice(out, sends[j - sizes[-1]], (0, place[1, half - sizes[-1] + j] * BLOCK))
    return out


def solution(mesh):
    placed = (P("inner", ("groups", "outer")), P("groups", None), P("groups"))
    return jax.shard_map(
        shards,
        mesh=mesh,
        in_specs=placed,
        out_specs=P("inner", ("groups", "outer")),
        check_vma=False,
    )
```

```python
import functools

import jax
import jax.numpy as jnp
from jax import lax
from jax.experimental import pallas as pl
from jax.experimental.pallas import tpu as pltpu
from jax.sharding import PartitionSpec as P

BLOCK = 128
STRETCH = 256
CHUNKS = (2, 2, 2, 2)
LAST = 4
LAG = 2

ANY = pl.BlockSpec(memory_space=pl.ANY)
HBM = pl.BlockSpec(memory_space=pltpu.HBM)
VMEM = pl.BlockSpec(memory_space=pltpu.VMEM)
SMEM = pl.BlockSpec(memory_space=pltpu.SMEM)


def column(ref, block):
    start = block * BLOCK
    if not isinstance(block, int):
        start = pl.multiple_of(start, BLOCK)
    return ref.at[:, pl.ds(start, BLOCK)]


def plan(per_dev, stride, blocks_ref, weight_ref, place_ref, scale_ref):
    me, owners = lax.axis_index("outer"), lax.axis_size("outer")
    half = per_dev // 2

    def mated(c, carry):
        first, second = blocks_ref[0, c], blocks_ref[1, c]
        first_mine = lax.div(first, per_dev) == me
        mine = jnp.where(first_mine, first, second)
        other = lax.rem(jnp.where(first_mine, second, first), per_dev)
        upper = me >= stride
        local = lax.rem(mine, per_dev)
        key = jnp.where(upper, local, other)
        spare = lax.div(mine, per_dev) != me
        keeps = (key >= half) == upper
        slot = lax.rem(key, half)
        kept = jnp.where(spare | jnp.logical_not(keeps), half, slot)
        place_ref[0, kept] = local
        scale_ref[0, kept] = 4.0 * weight_ref[c]
        place_ref[1, jnp.where(spare | keeps, half, slot)] = local
        return carry

    def one(c, counts):
        first, second = blocks_ref[0, c], blocks_ref[1, c]
        firsts, seconds = counts
        place_ref[0, firsts] = lax.rem(first, per_dev)
        scale_ref[0, firsts] = 4.0 * weight_ref[c]
        place_ref[1, seconds] = lax.rem(second, per_dev)
        firsts += (lax.div(first, per_dev) == me).astype(jnp.int32)
        seconds += (lax.div(second, per_dev) == me).astype(jnp.int32)
        return firsts, seconds

    if owners == 2 * stride:
        lax.fori_loop(0, blocks_ref.shape[1], mated, jnp.int32(0))
    else:
        lax.fori_loop(0, blocks_ref.shape[1], one, (jnp.int32(0), jnp.int32(0)))


def gather(decoder_ref, blocks, outs, sizes, sem):
    copies = []
    for size, out in zip(sizes, outs):
        for j in range(size):
            copies.append(
                pltpu.make_async_copy(
                    column(decoder_ref, blocks[len(copies)]), column(out, j), sem.at[len(copies)]
                )
            )
            copies[-1].start()
    for copy in copies:
        copy.wait()


def opening_kernel(per_dev, stride, sizes, blocks_ref, decoder_ref, out_ref, held_ref, sem):
    me, owners = lax.axis_index("outer"), lax.axis_size("outer")
    half = per_dev // 2

    def fetch():
        copy = pltpu.make_async_copy(blocks_ref, held_ref, sem.at[0])
        copy.start()
        copy.wait()

    if owners == 2 * stride:

        @pl.when(me >= stride)
        def _():
            copy = pltpu.make_async_copy(decoder_ref.at[:, pl.ds(0, sizes[0] * BLOCK)], out_ref, sem.at[0])
            copy.start()
            copy.wait()

        @pl.when(me < stride)
        def _():
            fetch()
            copies = []
            for j in range(sizes[0]):
                wanted = (me + stride) * per_dev + half + j
                mate = jnp.int32(0)
                for c in range(held_ref.shape[1]):
                    first, second = held_ref[0, c], held_ref[1, c]
                    mate = jnp.where(first == wanted, second, jnp.where(second == wanted, first, mate))
                copies.append(
                    pltpu.make_async_copy(column(decoder_ref, lax.rem(mate, per_dev)), column(out_ref, j), sem.at[j])
                )
                copies[-1].start()
            for copy in copies:
                copy.wait()

    else:
        fetch()
        blocks, c = [], jnp.int32(0)
        for _ in range(sizes[0]):
            c = lax.while_loop(lambda c: lax.div(held_ref[1, c], per_dev) != me, lambda c: c + 1, c)
            blocks.append(lax.rem(held_ref[1, c], per_dev))
            c += 1
        gather(decoder_ref, blocks, [out_ref], sizes, sem)


def planning_kernel(per_dev, stride, start, sizes, blocks_ref, weight_ref, decoder_ref, first_ref, place_ref, scale_ref, *rest):
    outs, sem = rest[:-1], rest[-1]
    plan(per_dev, stride, blocks_ref, weight_ref, place_ref, scale_ref)
    gather(decoder_ref, [place_ref[1, start + j] for j in range(sum(sizes))], outs, sizes, sem)


def gram_parts(x):
    gram = lax.dot_general(x, x, (((0,), (0,)), ((), ())), preferred_element_type=jnp.float32)
    row = lax.broadcasted_iota(jnp.int32, (BLOCK, BLOCK), 0)
    col = lax.broadcasted_iota(jnp.int32, (BLOCK, BLOCK), 1)
    own = jnp.where(row < col, gram[:BLOCK, :BLOCK], gram[BLOCK:, BLOCK:])
    return own, gram[:BLOCK, BLOCK:]


def tangents(x, own, cross, scale):
    row = lax.broadcasted_iota(jnp.int32, (BLOCK, BLOCK), 0)
    col = lax.broadcasted_iota(jnp.int32, (BLOCK, BLOCK), 1)
    upper = jnp.where(row < col, own, 0.0)
    lower = jnp.where(row > col, own, 0.0)
    gram = jnp.concatenate(
        [
            jnp.concatenate([upper + upper.T, cross], axis=1),
            jnp.concatenate([cross.T, lower + lower.T], axis=1),
        ],
        axis=0,
    )
    coef = (gram * scale).astype(jnp.bfloat16)
    along = jnp.sum(gram * coef.astype(jnp.float32), axis=0, keepdims=True)
    grad = jnp.dot(x, coef, preferred_element_type=jnp.float32).astype(jnp.bfloat16)
    return (grad.astype(jnp.float32) - along * x.astype(jnp.float32)).astype(jnp.bfloat16)


def step_kernel(spec, *refs):
    refs = list(refs)
    take = lambda: refs.pop(0)
    place_ref = take()
    scale_ref, decoder_ref = (None, None) if spec["lean"] else (take(), take())
    gram_in = take() if spec["gram"] else None
    final_in = take() if spec["final"] else None
    parts = [take() for _ in range(spec["ranks"])] if spec["final"] else None
    back_in = take() if spec["back"] else None
    for _ in range(spec["unread"]):
        take()
    gram_out = take() if spec["gram"] else None
    send_outs = [take() for _ in range(spec["sends"])]
    out_ref = take() if spec["final"] or spec["back"] else None
    gram_x, final_x, final_t, load_sem, move_sem, store_sem = (None,) * 4 + (refs[0], None) if spec["lean"] else refs

    loads = {}

    def load(kind, scratch, source, start, size):
        for j in range(size):
            pair = (
                pltpu.make_async_copy(
                    column(decoder_ref, place_ref[0, start + j]),
                    scratch.at[j, :, pl.ds(0, BLOCK)],
                    load_sem.at[len(loads), 0],
                ),
                pltpu.make_async_copy(
                    column(source, j), scratch.at[j, :, pl.ds(BLOCK, BLOCK)], load_sem.at[len(loads), 1]
                ),
            )
            for copy in pair:
                copy.start()
            loads[kind, j] = pair

    moves = []

    def move(source, target):
        moves.append(pltpu.make_async_copy(source, target, move_sem.at[len(moves)]))
        moves[-1].start()

    if spec["pack"]:
        start, size = spec["pack"]
        for j in range(size):
            move(column(decoder_ref, place_ref[1, start + j]), column(send_outs[0], j))
    if spec["gram"]:
        load("gram", gram_x, gram_in, *spec["gram"])
    if spec["final"]:
        load("final", final_x, final_in, *spec["final"])
    if spec["back"]:
        start, size = spec["back"]
        for j in range(size):
            move(column(back_in, j), column(out_ref, place_ref[1, start + j]))

    if spec["gram"]:
        for j in range(spec["gram"][1]):
            for copy in loads["gram", j]:
                copy.wait()
            gram_out[j, 0], gram_out[j, 1] = gram_parts(gram_x[j])

    stores = []
    if spec["final"]:
        start, size = spec["final"]
        for j in range(size):
            for copy in loads["final", j]:
                copy.wait()
            a, b, c, d = (part[j] for part in parts)
            total = (a + b) + (c + d)
            final_t[j] = tangents(final_x[j], total[0], total[1], scale_ref[0, start + j])
            everything = (0, final_t.shape[1])
            targets = [(column(out_ref, place_ref[0, start + j]), 0, everything)]
            if spec["pieces"]:
                targets += [
                    (out, BLOCK, rows) for out, (block, rows) in zip(send_outs, spec["pieces"]) if block == j
                ]
            else:
                targets.append((column(send_outs[0], j), BLOCK, everything))
            for target, side, rows in targets:
                stores.append(
                    pltpu.make_async_copy(
                        final_t.at[j, pl.ds(*rows), pl.ds(side, BLOCK)], target, store_sem.at[len(stores)]
                    )
                )
                stores[-1].start()
    for copy in moves + stores:
        copy.wait()


def shards(decoder, stretch_blocks, stretch_weight):
    width, columns = decoder.shape
    per_dev = columns // BLOCK
    half = per_dev // 2
    owners, ranks = lax.axis_size("outer"), lax.axis_size("inner")
    stride = min(owners, per_dev) // 2
    sizes = CHUNKS
    count = len(sizes)
    starts = [sum(sizes[:k]) for k in range(count)]
    chunk = lambda k: (starts[k], sizes[k])
    array = lambda k: jax.ShapeDtypeStruct((width, sizes[k] * BLOCK), decoder.dtype)
    out_shape = jax.ShapeDtypeStruct(decoder.shape, decoder.dtype)
    to_first = [(o, (o + stride) % owners) for o in range(owners)]
    to_second = [(o, (o - stride) % owners) for o in range(owners)]

    stay = lambda x: pltpu.with_memory_space_constraint(x, pltpu.HBM)
    pairs, decoder = stay(stretch_blocks.T), stay(decoder)
    first = pl.pallas_call(
        functools.partial(opening_kernel, per_dev, stride, sizes[:1]),
        out_shape=array(0),
        in_specs=[HBM, HBM],
        out_specs=ANY,
        scratch_shapes=[pltpu.SMEM(pairs.shape, jnp.int32), pltpu.SemaphoreType.DMA((sizes[0],))],
        compiler_params=pltpu.CompilerParams(vmem_limit_bytes=8 * 2**20),
        name="opening",
    )(pairs, decoder)
    place, scale, *raw = pl.pallas_call(
        functools.partial(planning_kernel, per_dev, stride, starts[1], sizes[1:LAG]),
        out_shape=[
            jax.ShapeDtypeStruct((2, half + 1), jnp.int32),
            jax.ShapeDtypeStruct((1, half + 1), jnp.float32),
        ]
        + [array(k) for k in range(1, LAG)],
        in_specs=[SMEM, SMEM, HBM, ANY],
        out_specs=[SMEM, SMEM] + [ANY] * (LAG - 1),
        scratch_shapes=[pltpu.SemaphoreType.DMA((per_dev,))],
        compiler_params=pltpu.CompilerParams(vmem_limit_bytes=8 * 2**20),
        name="planning",
    )(stretch_blocks.T, stretch_weight, decoder, first)

    sends = [lax.ppermute(part, "outer", to_first) for part in [first] + raw]
    last = width // LAST
    pieces = [(j, (0, width)) for j in range(sizes[-1] - 1)]
    pieces += [(sizes[-1] - 1, (0, width - last)), (sizes[-1] - 1, (width - last, last))]
    parts = {}
    out = chain = None
    for step in range(2 * count - 1):
        arrived = sends[step]
        gram = chunk(step) if step < count else None
        pack = chunk(step + LAG) if step + LAG < count else None
        turn = step + LAG - count
        final = chunk(turn) if 0 <= turn < count else None
        back = chunk(step - count) if step >= count else None
        spec = {"gram": gram, "pack": pack, "final": final, "back": back, "ranks": ranks, "unread": 0}
        spec["lean"] = not (gram or pack or final)
        args, specs = [place], [SMEM]
        if not spec["lean"]:
            args, specs = args + [scale, decoder], specs + [SMEM, HBM]
        shapes, out_specs, aliases = [], [], {}
        if gram:
            args, specs = args + [arrived], specs + [ANY]
            shapes.append(jax.ShapeDtypeStruct((gram[1], 2, BLOCK, BLOCK), jnp.float32))
            out_specs.append(VMEM)
        if final:
            args, specs = args + [sends[turn]] + parts.pop(turn), specs + [ANY] + [VMEM] * ranks
        if back:
            args, specs = args + [arrived], specs + [ANY]
        spec["sends"], spec["pieces"] = int(bool(final or pack)), None
        if turn == count - 1:
            spec["sends"], spec["pieces"] = len(pieces), pieces
            shapes += [jax.ShapeDtypeStruct((size, BLOCK), decoder.dtype) for _, (_, size) in pieces]
            out_specs += [ANY] * len(pieces)
        elif final or pack:
            shapes.append(array(turn if final else step + LAG))
            out_specs.append(ANY)
        if final or back:
            if out is not None:
                aliases = {len(args): len(shapes)}
                args, specs, chain = args + [out], specs + [ANY], None
                spec["unread"] += 1
            shapes.append(out_shape)
            out_specs.append(ANY)
        if chain is not None:
            args, specs = args + [chain], specs + [ANY]
            spec["unread"] += 1
        slot = max(sizes)
        results = list(
            pl.pallas_call(
                functools.partial(step_kernel, spec),
                out_shape=shapes,
                in_specs=specs,
                out_specs=out_specs,
                input_output_aliases=aliases,
                scratch_shapes=[pltpu.SemaphoreType.DMA((2 * slot,))]
                if spec["lean"]
                else [
                    pltpu.VMEM((slot, width, STRETCH), decoder.dtype),
                    pltpu.VMEM((slot, width, STRETCH), decoder.dtype),
                    pltpu.VMEM((slot, width, STRETCH), decoder.dtype),
                    pltpu.SemaphoreType.DMA((2 * slot, 2)),
                    pltpu.SemaphoreType.DMA((2 * slot,)),
                    pltpu.SemaphoreType.DMA((2 * slot + 1,)),
                ],
                compiler_params=pltpu.CompilerParams(vmem_limit_bytes=32 * 2**20),
                name="step",
            )(*args)
        )
        if gram:
            chain = mine = results.pop(0)
            parts[step] = [mine] + [
                lax.ppermute(mine, "inner", [(i, i ^ hop) for i in range(ranks)]) for hop in range(1, ranks)
            ]
        for _ in range(spec["sends"]):
            sends.append(lax.ppermute(results.pop(0), "outer", to_second if final else to_first))
        if final or back:
            out = results.pop(0)
    for piece, (block, rows) in zip(sends[-len(pieces) :], pieces):
        out = lax.dynamic_update_slice(out, piece, (rows[0], place[1, starts[-1] + block] * BLOCK))
    return out


def solution(mesh):
    placed = (P("inner", ("groups", "outer")), P("groups", None), P("groups"))
    return jax.shard_map(
        shards,
        mesh=mesh,
        in_specs=placed,
        out_specs=P("inner", ("groups", "outer")),
        check_vma=False,
    )
```

```python
import functools

import jax
import jax.numpy as jnp
from jax import lax
from jax.experimental import pallas as pl
from jax.experimental.pallas import tpu as pltpu
from jax.sharding import PartitionSpec as P

BLOCK = 128
STRETCH = 256
CHUNKS = (2, 2, 2, 2)
LAST = 4
LAG = 2

ANY = pl.BlockSpec(memory_space=pl.ANY)
HBM = pl.BlockSpec(memory_space=pltpu.HBM)
VMEM = pl.BlockSpec(memory_space=pltpu.VMEM)
SMEM = pl.BlockSpec(memory_space=pltpu.SMEM)


def column(ref, block):
    start = block * BLOCK
    if not isinstance(block, int):
        start = pl.multiple_of(start, BLOCK)
    return ref.at[:, pl.ds(start, BLOCK)]


def plan(per_dev, stride, blocks_ref, weight_ref, place_ref, scale_ref):
    me, owners = lax.axis_index("outer"), lax.axis_size("outer")
    half = per_dev // 2

    def mated(c, carry):
        first, second = blocks_ref[0, c], blocks_ref[1, c]
        first_mine = lax.div(first, per_dev) == me
        mine = jnp.where(first_mine, first, second)
        other = lax.rem(jnp.where(first_mine, second, first), per_dev)
        upper = me >= stride
        local = lax.rem(mine, per_dev)
        key = jnp.where(upper, local, other)
        spare = lax.div(mine, per_dev) != me
        keeps = (key >= half) == upper
        slot = lax.rem(key, half)
        kept = jnp.where(spare | jnp.logical_not(keeps), half, slot)
        place_ref[0, kept] = local
        scale_ref[0, kept] = 4.0 * weight_ref[c]
        place_ref[1, jnp.where(spare | keeps, half, slot)] = local
        return carry

    def one(c, counts):
        first, second = blocks_ref[0, c], blocks_ref[1, c]
        firsts, seconds = counts
        place_ref[0, firsts] = lax.rem(first, per_dev)
        scale_ref[0, firsts] = 4.0 * weight_ref[c]
        place_ref[1, seconds] = lax.rem(second, per_dev)
        firsts += (lax.div(first, per_dev) == me).astype(jnp.int32)
        seconds += (lax.div(second, per_dev) == me).astype(jnp.int32)
        return firsts, seconds

    if owners == 2 * stride:
        lax.fori_loop(0, blocks_ref.shape[1], mated, jnp.int32(0))
    else:
        lax.fori_loop(0, blocks_ref.shape[1], one, (jnp.int32(0), jnp.int32(0)))


def gather(decoder_ref, blocks, outs, sizes, sem):
    copies = []
    for size, out in zip(sizes, outs):
        for j in range(size):
            copies.append(
                pltpu.make_async_copy(
                    column(decoder_ref, blocks[len(copies)]), column(out, j), sem.at[len(copies)]
                )
            )
            copies[-1].start()
    for copy in copies:
        copy.wait()


def opening_kernel(per_dev, stride, sizes, blocks_ref, decoder_ref, out_ref, held_ref, sem):
    me, owners = lax.axis_index("outer"), lax.axis_size("outer")
    half = per_dev // 2

    def fetch():
        copy = pltpu.make_async_copy(blocks_ref, held_ref, sem.at[0])
        copy.start()
        copy.wait()

    if owners == 2 * stride:

        @pl.when(me >= stride)
        def _():
            copy = pltpu.make_async_copy(decoder_ref.at[:, pl.ds(0, sizes[0] * BLOCK)], out_ref, sem.at[0])
            copy.start()
            copy.wait()

        @pl.when(me < stride)
        def _():
            fetch()
            copies = []
            for j in range(sizes[0]):
                wanted = (me + stride) * per_dev + half + j
                mate = jnp.int32(0)
                for c in range(held_ref.shape[1]):
                    first, second = held_ref[0, c], held_ref[1, c]
                    mate = jnp.where(first == wanted, second, jnp.where(second == wanted, first, mate))
                copies.append(
                    pltpu.make_async_copy(column(decoder_ref, lax.rem(mate, per_dev)), column(out_ref, j), sem.at[j])
                )
                copies[-1].start()
            for copy in copies:
                copy.wait()

    else:
        fetch()
        blocks, c = [], jnp.int32(0)
        for _ in range(sizes[0]):
            c = lax.while_loop(lambda c: lax.div(held_ref[1, c], per_dev) != me, lambda c: c + 1, c)
            blocks.append(lax.rem(held_ref[1, c], per_dev))
            c += 1
        gather(decoder_ref, blocks, [out_ref], sizes, sem)


def planning_kernel(per_dev, stride, start, sizes, blocks_ref, weight_ref, decoder_ref, first_ref, place_ref, scale_ref, *rest):
    outs, sem = rest[:-1], rest[-1]
    plan(per_dev, stride, blocks_ref, weight_ref, place_ref, scale_ref)
    gather(decoder_ref, [place_ref[1, start + j] for j in range(sum(sizes))], outs, sizes, sem)


def gram_parts(x):
    gram = lax.dot_general(x, x, (((0,), (0,)), ((), ())), preferred_element_type=jnp.float32)
    row = lax.broadcasted_iota(jnp.int32, (BLOCK, BLOCK), 0)
    col = lax.broadcasted_iota(jnp.int32, (BLOCK, BLOCK), 1)
    own = jnp.where(row < col, gram[:BLOCK, :BLOCK], gram[BLOCK:, BLOCK:])
    return own, gram[:BLOCK, BLOCK:]


def tangents(x, own, cross, scale):
    row = lax.broadcasted_iota(jnp.int32, (BLOCK, BLOCK), 0)
    col = lax.broadcasted_iota(jnp.int32, (BLOCK, BLOCK), 1)
    upper = jnp.where(row < col, own, 0.0)
    lower = jnp.where(row > col, own, 0.0)
    gram = jnp.concatenate(
        [
            jnp.concatenate([upper + upper.T, cross], axis=1),
            jnp.concatenate([cross.T, lower + lower.T], axis=1),
        ],
        axis=0,
    )
    coef = (gram * scale).astype(jnp.bfloat16)
    along = jnp.sum(gram * coef.astype(jnp.float32), axis=0, keepdims=True)
    grad = jnp.dot(x, coef, preferred_element_type=jnp.float32).astype(jnp.bfloat16)
    return (grad.astype(jnp.float32) - along * x.astype(jnp.float32)).astype(jnp.bfloat16)


def step_kernel(spec, *refs):
    refs = list(refs)
    take = lambda: refs.pop(0)
    place_ref = take()
    scale_ref, decoder_ref = (None, None) if spec["lean"] else (take(), take())
    gram_in = take() if spec["gram"] else None
    final_in = take() if spec["final"] else None
    parts = [take() for _ in range(spec["ranks"])] if spec["final"] else None
    back_in = take() if spec["back"] else None
    for _ in range(spec["unread"]):
        take()
    gram_out = take() if spec["gram"] else None
    send_outs = [take() for _ in range(spec["sends"])]
    out_ref = take() if spec["final"] or spec["back"] else None
    gram_x, final_x, final_t, load_sem, move_sem, store_sem = (None,) * 4 + (refs[0], None) if spec["lean"] else refs

    loads = {}

    def load(kind, scratch, source, start, size):
        for j in range(size):
            pair = (
                pltpu.make_async_copy(
                    column(decoder_ref, place_ref[0, start + j]),
                    scratch.at[j, :, pl.ds(0, BLOCK)],
                    load_sem.at[len(loads), 0],
                ),
                pltpu.make_async_copy(
                    column(source, j), scratch.at[j, :, pl.ds(BLOCK, BLOCK)], load_sem.at[len(loads), 1]
                ),
            )
            for copy in pair:
                copy.start()
            loads[kind, j] = pair

    moves = []

    def move(source, target):
        moves.append(pltpu.make_async_copy(source, target, move_sem.at[len(moves)]))
        moves[-1].start()

    if spec["pack"]:
        start, size = spec["pack"]
        for j in range(size):
            move(column(decoder_ref, place_ref[1, start + j]), column(send_outs[0], j))
    if spec["gram"]:
        load("gram", gram_x, gram_in, *spec["gram"])
    if spec["final"]:
        load("final", final_x, final_in, *spec["final"])
    if spec["back"]:
        start, size = spec["back"]
        for j in range(size):
            move(column(back_in, j), column(out_ref, place_ref[1, start + j]))

    if spec["gram"]:
        for j in range(spec["gram"][1]):
            for copy in loads["gram", j]:
                copy.wait()
            gram_out[j, 0], gram_out[j, 1] = gram_parts(gram_x[j])

    stores = []
    if spec["final"]:
        start, size = spec["final"]
        for j in range(size):
            for copy in loads["final", j]:
                copy.wait()
            a, b, c, d = (part[j] for part in parts)
            total = (a + b) + (c + d)
            final_t[j] = tangents(final_x[j], total[0], total[1], scale_ref[0, start + j])
            everything = (0, final_t.shape[1])
            targets = [(column(out_ref, place_ref[0, start + j]), 0, everything)]
            if spec["pieces"]:
                targets += [
                    (out, BLOCK, rows) for out, (block, rows) in zip(send_outs, spec["pieces"]) if block == j
                ]
            else:
                targets.append((column(send_outs[0], j), BLOCK, everything))
            for target, side, rows in targets:
                stores.append(
                    pltpu.make_async_copy(
                        final_t.at[j, pl.ds(*rows), pl.ds(side, BLOCK)], target, store_sem.at[len(stores)]
                    )
                )
                stores[-1].start()
    for copy in moves + stores:
        copy.wait()


def shards(decoder, stretch_blocks, stretch_weight):
    width, columns = decoder.shape
    per_dev = columns // BLOCK
    half = per_dev // 2
    owners, ranks = lax.axis_size("outer"), lax.axis_size("inner")
    stride = min(owners, per_dev) // 2
    sizes = CHUNKS
    count = len(sizes)
    starts = [sum(sizes[:k]) for k in range(count)]
    chunk = lambda k: (starts[k], sizes[k])
    array = lambda k: jax.ShapeDtypeStruct((width, sizes[k] * BLOCK), decoder.dtype)
    out_shape = jax.ShapeDtypeStruct(decoder.shape, decoder.dtype)
    to_first = [(o, (o + stride) % owners) for o in range(owners)]
    to_second = [(o, (o - stride) % owners) for o in range(owners)]

    stay = lambda x: pltpu.with_memory_space_constraint(x, pltpu.HBM)
    pairs, decoder = stay(stretch_blocks.T), stay(decoder)
    first = pl.pallas_call(
        functools.partial(opening_kernel, per_dev, stride, sizes[:1]),
        out_shape=array(0),
        in_specs=[HBM, HBM],
        out_specs=ANY,
        scratch_shapes=[pltpu.SMEM(pairs.shape, jnp.int32), pltpu.SemaphoreType.DMA((sizes[0],))],
        compiler_params=pltpu.CompilerParams(vmem_limit_bytes=8 * 2**20),
        name="opening",
    )(pairs, decoder)
    place, scale, *raw = pl.pallas_call(
        functools.partial(planning_kernel, per_dev, stride, starts[1], sizes[1:LAG]),
        out_shape=[
            jax.ShapeDtypeStruct((2, half + 1), jnp.int32),
            jax.ShapeDtypeStruct((1, half + 1), jnp.float32),
        ]
        + [array(k) for k in range(1, LAG)],
        in_specs=[SMEM, SMEM, HBM, ANY],
        out_specs=[SMEM, SMEM] + [ANY] * (LAG - 1),
        scratch_shapes=[pltpu.SemaphoreType.DMA((per_dev,))],
        compiler_params=pltpu.CompilerParams(vmem_limit_bytes=8 * 2**20),
        name="planning",
    )(pairs, stay(stretch_weight), decoder, first)

    sends = [lax.ppermute(part, "outer", to_first) for part in [first] + raw]
    last = width // LAST
    pieces = [(j, (0, width)) for j in range(sizes[-1] - 1)]
    pieces += [(sizes[-1] - 1, (0, width - last)), (sizes[-1] - 1, (width - last, last))]
    parts = {}
    out = chain = None
    for step in range(2 * count - 1):
        arrived = sends[step]
        gram = chunk(step) if step < count else None
        pack = chunk(step + LAG) if step + LAG < count else None
        turn = step + LAG - count
        final = chunk(turn) if 0 <= turn < count else None
        back = chunk(step - count) if step >= count else None
        spec = {"gram": gram, "pack": pack, "final": final, "back": back, "ranks": ranks, "unread": 0}
        spec["lean"] = not (gram or pack or final)
        args, specs = [place], [SMEM]
        if not spec["lean"]:
            args, specs = args + [scale, decoder], specs + [SMEM, HBM]
        shapes, out_specs, aliases = [], [], {}
        if gram:
            args, specs = args + [arrived], specs + [ANY]
            shapes.append(jax.ShapeDtypeStruct((gram[1], 2, BLOCK, BLOCK), jnp.float32))
            out_specs.append(VMEM)
        if final:
            args, specs = args + [sends[turn]] + parts.pop(turn), specs + [ANY] + [VMEM] * ranks
        if back:
            args, specs = args + [arrived], specs + [ANY]
        spec["sends"], spec["pieces"] = int(bool(final or pack)), None
        if turn == count - 1:
            spec["sends"], spec["pieces"] = len(pieces), pieces
            shapes += [jax.ShapeDtypeStruct((size, BLOCK), decoder.dtype) for _, (_, size) in pieces]
            out_specs += [ANY] * len(pieces)
        elif final or pack:
            shapes.append(array(turn if final else step + LAG))
            out_specs.append(ANY)
        if final or back:
            if out is not None:
                aliases = {len(args): len(shapes)}
                args, specs, chain = args + [out], specs + [ANY], None
                spec["unread"] += 1
            shapes.append(out_shape)
            out_specs.append(ANY)
        if chain is not None:
            args, specs = args + [chain], specs + [ANY]
            spec["unread"] += 1
        slot = max(sizes)
        results = list(
            pl.pallas_call(
                functools.partial(step_kernel, spec),
                out_shape=shapes,
                in_specs=specs,
                out_specs=out_specs,
                input_output_aliases=aliases,
                scratch_shapes=[pltpu.SemaphoreType.DMA((2 * slot,))]
                if spec["lean"]
                else [
                    pltpu.VMEM((slot, width, STRETCH), decoder.dtype),
                    pltpu.VMEM((slot, width, STRETCH), decoder.dtype),
                    pltpu.VMEM((slot, width, STRETCH), decoder.dtype),
                    pltpu.SemaphoreType.DMA((2 * slot, 2)),
                    pltpu.SemaphoreType.DMA((2 * slot,)),
                    pltpu.SemaphoreType.DMA((2 * slot + 1,)),
                ],
                compiler_params=pltpu.CompilerParams(vmem_limit_bytes=32 * 2**20),
                name="step",
            )(*args)
        )
        if gram:
            chain = mine = results.pop(0)
            parts[step] = [mine] + [
                lax.ppermute(mine, "inner", [(i, i ^ hop) for i in range(ranks)]) for hop in range(1, ranks)
            ]
        for _ in range(spec["sends"]):
            sends.append(lax.ppermute(results.pop(0), "outer", to_second if final else to_first))
        if final or back:
            out = results.pop(0)
    for piece, (block, rows) in zip(sends[-len(pieces) :], pieces):
        out = lax.dynamic_update_slice(out, piece, (rows[0], place[1, starts[-1] + block] * BLOCK))
    return out


def solution(mesh):
    placed = (P("inner", ("groups", "outer")), P("groups", None), P("groups"))
    return jax.shard_map(
        shards,
        mesh=mesh,
        in_specs=placed,
        out_specs=P("inner", ("groups", "outer")),
        check_vma=False,
    )
```

```python
import functools

import jax
import jax.numpy as jnp
from jax import lax
from jax.experimental import pallas as pl
from jax.experimental.pallas import tpu as pltpu
from jax.sharding import PartitionSpec as P

BLOCK = 128
STRETCH = 256
CHUNKS = (2, 3, 3)
LAST = 4
LAG = 2

ANY = pl.BlockSpec(memory_space=pl.ANY)
HBM = pl.BlockSpec(memory_space=pltpu.HBM)
VMEM = pl.BlockSpec(memory_space=pltpu.VMEM)
SMEM = pl.BlockSpec(memory_space=pltpu.SMEM)


def column(ref, block):
    start = block * BLOCK
    if not isinstance(block, int):
        start = pl.multiple_of(start, BLOCK)
    return ref.at[:, pl.ds(start, BLOCK)]


def plan(per_dev, stride, blocks_ref, weight_ref, place_ref, scale_ref):
    me, owners = lax.axis_index("outer"), lax.axis_size("outer")
    half = per_dev // 2

    def mated(c, carry):
        first, second = blocks_ref[0, c], blocks_ref[1, c]
        first_mine = lax.div(first, per_dev) == me
        mine = jnp.where(first_mine, first, second)
        other = lax.rem(jnp.where(first_mine, second, first), per_dev)
        upper = me >= stride
        local = lax.rem(mine, per_dev)
        key = jnp.where(upper, local, other)
        spare = lax.div(mine, per_dev) != me
        keeps = (key >= half) == upper
        slot = lax.rem(key, half)
        kept = jnp.where(spare | jnp.logical_not(keeps), half, slot)
        place_ref[0, kept] = local
        scale_ref[0, kept] = 4.0 * weight_ref[c]
        place_ref[1, jnp.where(spare | keeps, half, slot)] = local
        return carry

    def one(c, counts):
        first, second = blocks_ref[0, c], blocks_ref[1, c]
        firsts, seconds = counts
        place_ref[0, firsts] = lax.rem(first, per_dev)
        scale_ref[0, firsts] = 4.0 * weight_ref[c]
        place_ref[1, seconds] = lax.rem(second, per_dev)
        firsts += (lax.div(first, per_dev) == me).astype(jnp.int32)
        seconds += (lax.div(second, per_dev) == me).astype(jnp.int32)
        return firsts, seconds

    if owners == 2 * stride:
        lax.fori_loop(0, blocks_ref.shape[1], mated, jnp.int32(0))
    else:
        lax.fori_loop(0, blocks_ref.shape[1], one, (jnp.int32(0), jnp.int32(0)))


def gather(decoder_ref, blocks, outs, sizes, sem):
    copies = []
    for size, out in zip(sizes, outs):
        for j in range(size):
            copies.append(
                pltpu.make_async_copy(
                    column(decoder_ref, blocks[len(copies)]), column(out, j), sem.at[len(copies)]
                )
            )
            copies[-1].start()
    for copy in copies:
        copy.wait()


def opening_kernel(per_dev, stride, sizes, blocks_ref, decoder_ref, out_ref, held_ref, sem):
    me, owners = lax.axis_index("outer"), lax.axis_size("outer")
    half = per_dev // 2

    def fetch():
        copy = pltpu.make_async_copy(blocks_ref, held_ref, sem.at[0])
        copy.start()
        copy.wait()

    if owners == 2 * stride:

        @pl.when(me >= stride)
        def _():
            copy = pltpu.make_async_copy(decoder_ref.at[:, pl.ds(0, sizes[0] * BLOCK)], out_ref, sem.at[0])
            copy.start()
            copy.wait()

        @pl.when(me < stride)
        def _():
            fetch()
            copies = []
            for j in range(sizes[0]):
                wanted = (me + stride) * per_dev + half + j
                mate = jnp.int32(0)
                for c in range(held_ref.shape[1]):
                    first, second = held_ref[0, c], held_ref[1, c]
                    mate = jnp.where(first == wanted, second, jnp.where(second == wanted, first, mate))
                copies.append(
                    pltpu.make_async_copy(column(decoder_ref, lax.rem(mate, per_dev)), column(out_ref, j), sem.at[j])
                )
                copies[-1].start()
            for copy in copies:
                copy.wait()

    else:
        fetch()
        blocks, c = [], jnp.int32(0)
        for _ in range(sizes[0]):
            c = lax.while_loop(lambda c: lax.div(held_ref[1, c], per_dev) != me, lambda c: c + 1, c)
            blocks.append(lax.rem(held_ref[1, c], per_dev))
            c += 1
        gather(decoder_ref, blocks, [out_ref], sizes, sem)


def planning_kernel(per_dev, stride, start, sizes, blocks_ref, weight_ref, decoder_ref, first_ref, place_ref, scale_ref, *rest):
    outs, sem = rest[:-1], rest[-1]
    plan(per_dev, stride, blocks_ref, weight_ref, place_ref, scale_ref)
    gather(decoder_ref, [place_ref[1, start + j] for j in range(sum(sizes))], outs, sizes, sem)


def gram_parts(x):
    gram = lax.dot_general(x, x, (((0,), (0,)), ((), ())), preferred_element_type=jnp.float32)
    row = lax.broadcasted_iota(jnp.int32, (BLOCK, BLOCK), 0)
    col = lax.broadcasted_iota(jnp.int32, (BLOCK, BLOCK), 1)
    own = jnp.where(row < col, gram[:BLOCK, :BLOCK], gram[BLOCK:, BLOCK:])
    return own, gram[:BLOCK, BLOCK:]


def tangents(x, own, cross, scale):
    row = lax.broadcasted_iota(jnp.int32, (BLOCK, BLOCK), 0)
    col = lax.broadcasted_iota(jnp.int32, (BLOCK, BLOCK), 1)
    upper = jnp.where(row < col, own, 0.0)
    lower = jnp.where(row > col, own, 0.0)
    gram = jnp.concatenate(
        [
            jnp.concatenate([upper + upper.T, cross], axis=1),
            jnp.concatenate([cross.T, lower + lower.T], axis=1),
        ],
        axis=0,
    )
    coef = (gram * scale).astype(jnp.bfloat16)
    along = jnp.sum(gram * coef.astype(jnp.float32), axis=0, keepdims=True)
    grad = jnp.dot(x, coef, preferred_element_type=jnp.float32).astype(jnp.bfloat16)
    return (grad.astype(jnp.float32) - along * x.astype(jnp.float32)).astype(jnp.bfloat16)


def step_kernel(spec, *refs):
    refs = list(refs)
    take = lambda: refs.pop(0)
    place_ref = take()
    scale_ref, decoder_ref = (None, None) if spec["lean"] else (take(), take())
    gram_in = take() if spec["gram"] else None
    final_in = take() if spec["final"] else None
    parts = [take() for _ in range(spec["ranks"])] if spec["final"] else None
    back_in = take() if spec["back"] else None
    for _ in range(spec["unread"]):
        take()
    gram_out = take() if spec["gram"] else None
    send_outs = [take() for _ in range(spec["sends"])]
    out_ref = take() if spec["final"] or spec["back"] else None
    gram_x, final_x, final_t, load_sem, move_sem, store_sem = (None,) * 4 + (refs[0], None) if spec["lean"] else refs

    loads = {}

    def load(kind, scratch, source, start, size):
        for j in range(size):
            pair = (
                pltpu.make_async_copy(
                    column(decoder_ref, place_ref[0, start + j]),
                    scratch.at[j, :, pl.ds(0, BLOCK)],
                    load_sem.at[len(loads), 0],
                ),
                pltpu.make_async_copy(
                    column(source, j), scratch.at[j, :, pl.ds(BLOCK, BLOCK)], load_sem.at[len(loads), 1]
                ),
            )
            for copy in pair:
                copy.start()
            loads[kind, j] = pair

    moves = []

    def move(source, target):
        moves.append(pltpu.make_async_copy(source, target, move_sem.at[len(moves)]))
        moves[-1].start()

    if spec["pack"]:
        start, size = spec["pack"]
        for j in range(size):
            move(column(decoder_ref, place_ref[1, start + j]), column(send_outs[0], j))
    if spec["gram"]:
        load("gram", gram_x, gram_in, *spec["gram"])
    if spec["final"]:
        load("final", final_x, final_in, *spec["final"])
    if spec["back"]:
        start, size = spec["back"]
        for j in range(size):
            move(column(back_in, j), column(out_ref, place_ref[1, start + j]))

    if spec["gram"]:
        for j in range(spec["gram"][1]):
            for copy in loads["gram", j]:
                copy.wait()
            gram_out[j, 0], gram_out[j, 1] = gram_parts(gram_x[j])

    stores = []
    if spec["final"]:
        start, size = spec["final"]
        for j in range(size):
            for copy in loads["final", j]:
                copy.wait()
            a, b, c, d = (part[j] for part in parts)
            total = (a + b) + (c + d)
            final_t[j] = tangents(final_x[j], total[0], total[1], scale_ref[0, start + j])
            everything = (0, final_t.shape[1])
            targets = [(column(out_ref, place_ref[0, start + j]), 0, everything)]
            if spec["pieces"]:
                targets += [
                    (out, BLOCK, rows) for out, (block, rows) in zip(send_outs, spec["pieces"]) if block == j
                ]
            else:
                targets.append((column(send_outs[0], j), BLOCK, everything))
            for target, side, rows in targets:
                stores.append(
                    pltpu.make_async_copy(
                        final_t.at[j, pl.ds(*rows), pl.ds(side, BLOCK)], target, store_sem.at[len(stores)]
                    )
                )
                stores[-1].start()
    for copy in moves + stores:
        copy.wait()


def shards(decoder, stretch_blocks, stretch_weight):
    width, columns = decoder.shape
    per_dev = columns // BLOCK
    half = per_dev // 2
    owners, ranks = lax.axis_size("outer"), lax.axis_size("inner")
    stride = min(owners, per_dev) // 2
    sizes = CHUNKS
    count = len(sizes)
    starts = [sum(sizes[:k]) for k in range(count)]
    chunk = lambda k: (starts[k], sizes[k])
    array = lambda k: jax.ShapeDtypeStruct((width, sizes[k] * BLOCK), decoder.dtype)
    out_shape = jax.ShapeDtypeStruct(decoder.shape, decoder.dtype)
    to_first = [(o, (o + stride) % owners) for o in range(owners)]
    to_second = [(o, (o - stride) % owners) for o in range(owners)]

    stay = lambda x: pltpu.with_memory_space_constraint(x, pltpu.HBM)
    pairs, decoder = stay(stretch_blocks.T), stay(decoder)
    first = pl.pallas_call(
        functools.partial(opening_kernel, per_dev, stride, sizes[:1]),
        out_shape=array(0),
        in_specs=[HBM, HBM],
        out_specs=ANY,
        scratch_shapes=[pltpu.SMEM(pairs.shape, jnp.int32), pltpu.SemaphoreType.DMA((sizes[0],))],
        compiler_params=pltpu.CompilerParams(vmem_limit_bytes=8 * 2**20),
        name="opening",
    )(pairs, decoder)
    place, scale, *raw = pl.pallas_call(
        functools.partial(planning_kernel, per_dev, stride, starts[1], sizes[1:LAG]),
        out_shape=[
            jax.ShapeDtypeStruct((2, half + 1), jnp.int32),
            jax.ShapeDtypeStruct((1, half + 1), jnp.float32),
        ]
        + [array(k) for k in range(1, LAG)],
        in_specs=[SMEM, SMEM, HBM, ANY],
        out_specs=[SMEM, SMEM] + [ANY] * (LAG - 1),
        scratch_shapes=[pltpu.SemaphoreType.DMA((per_dev,))],
        compiler_params=pltpu.CompilerParams(vmem_limit_bytes=8 * 2**20),
        name="planning",
    )(pairs, stay(stretch_weight), decoder, first)

    sends = [lax.ppermute(part, "outer", to_first) for part in [first] + raw]
    last = width // LAST
    pieces = [(j, (0, width)) for j in range(sizes[-1] - 1)]
    pieces += [(sizes[-1] - 1, (0, width - last)), (sizes[-1] - 1, (width - last, last))]
    parts = {}
    out = chain = None
    for step in range(2 * count - 1):
        arrived = sends[step]
        gram = chunk(step) if step < count else None
        pack = chunk(step + LAG) if step + LAG < count else None
        turn = step + LAG - count
        final = chunk(turn) if 0 <= turn < count else None
        back = chunk(step - count) if step >= count else None
        spec = {"gram": gram, "pack": pack, "final": final, "back": back, "ranks": ranks, "unread": 0}
        spec["lean"] = not (gram or pack or final)
        args, specs = [place], [SMEM]
        if not spec["lean"]:
            args, specs = args + [scale, decoder], specs + [SMEM, HBM]
        shapes, out_specs, aliases = [], [], {}
        if gram:
            args, specs = args + [arrived], specs + [ANY]
            shapes.append(jax.ShapeDtypeStruct((gram[1], 2, BLOCK, BLOCK), jnp.float32))
            out_specs.append(VMEM)
        if final:
            args, specs = args + [sends[turn]] + parts.pop(turn), specs + [ANY] + [VMEM] * ranks
        if back:
            args, specs = args + [arrived], specs + [ANY]
        spec["sends"], spec["pieces"] = int(bool(final or pack)), None
        if turn == count - 1:
            spec["sends"], spec["pieces"] = len(pieces), pieces
            shapes += [jax.ShapeDtypeStruct((size, BLOCK), decoder.dtype) for _, (_, size) in pieces]
            out_specs += [ANY] * len(pieces)
        elif final or pack:
            shapes.append(array(turn if final else step + LAG))
            out_specs.append(ANY)
        if final or back:
            if out is not None:
                aliases = {len(args): len(shapes)}
                args, specs, chain = args + [out], specs + [ANY], None
                spec["unread"] += 1
            shapes.append(out_shape)
            out_specs.append(ANY)
        if chain is not None:
            args, specs = args + [chain], specs + [ANY]
            spec["unread"] += 1
        slot = max(sizes)
        results = list(
            pl.pallas_call(
                functools.partial(step_kernel, spec),
                out_shape=shapes,
                in_specs=specs,
                out_specs=out_specs,
                input_output_aliases=aliases,
                scratch_shapes=[pltpu.SemaphoreType.DMA((2 * slot,))]
                if spec["lean"]
                else [
                    pltpu.VMEM((slot, width, STRETCH), decoder.dtype),
                    pltpu.VMEM((slot, width, STRETCH), decoder.dtype),
                    pltpu.VMEM((slot, width, STRETCH), decoder.dtype),
                    pltpu.SemaphoreType.DMA((2 * slot, 2)),
                    pltpu.SemaphoreType.DMA((2 * slot,)),
                    pltpu.SemaphoreType.DMA((2 * slot + 1,)),
                ],
                compiler_params=pltpu.CompilerParams(vmem_limit_bytes=32 * 2**20),
                name="step",
            )(*args)
        )
        if gram:
            chain = mine = results.pop(0)
            parts[step] = [mine] + [
                lax.ppermute(mine, "inner", [(i, i ^ hop) for i in range(ranks)]) for hop in range(1, ranks)
            ]
        for _ in range(spec["sends"]):
            sends.append(lax.ppermute(results.pop(0), "outer", to_second if final else to_first))
        if final or back:
            out = results.pop(0)
    for piece, (block, rows) in zip(sends[-len(pieces) :], pieces):
        out = lax.dynamic_update_slice(out, piece, (rows[0], place[1, starts[-1] + block] * BLOCK))
    return out


def solution(mesh):
    placed = (P("inner", ("groups", "outer")), P("groups", None), P("groups"))
    return jax.shard_map(
        shards,
        mesh=mesh,
        in_specs=placed,
        out_specs=P("inner", ("groups", "outer")),
        check_vma=False,
    )
```

```python
import functools

import jax
import jax.numpy as jnp
from jax import lax
from jax.experimental import pallas as pl
from jax.experimental.pallas import tpu as pltpu
from jax.sharding import PartitionSpec as P

BLOCK = 128
STRETCH = 256
CHUNKS = (2, 2, 2, 2)
LAST = 2
LAG = 2

ANY = pl.BlockSpec(memory_space=pl.ANY)
HBM = pl.BlockSpec(memory_space=pltpu.HBM)
VMEM = pl.BlockSpec(memory_space=pltpu.VMEM)
SMEM = pl.BlockSpec(memory_space=pltpu.SMEM)


def column(ref, block):
    start = block * BLOCK
    if not isinstance(block, int):
        start = pl.multiple_of(start, BLOCK)
    return ref.at[:, pl.ds(start, BLOCK)]


def plan(per_dev, stride, blocks_ref, weight_ref, place_ref, scale_ref):
    me, owners = lax.axis_index("outer"), lax.axis_size("outer")
    half = per_dev // 2

    def mated(c, carry):
        first, second = blocks_ref[0, c], blocks_ref[1, c]
        first_mine = lax.div(first, per_dev) == me
        mine = jnp.where(first_mine, first, second)
        other = lax.rem(jnp.where(first_mine, second, first), per_dev)
        upper = me >= stride
        local = lax.rem(mine, per_dev)
        key = jnp.where(upper, local, other)
        spare = lax.div(mine, per_dev) != me
        keeps = (key >= half) == upper
        slot = lax.rem(key, half)
        kept = jnp.where(spare | jnp.logical_not(keeps), half, slot)
        place_ref[0, kept] = local
        scale_ref[0, kept] = 4.0 * weight_ref[c]
        place_ref[1, jnp.where(spare | keeps, half, slot)] = local
        return carry

    def one(c, counts):
        first, second = blocks_ref[0, c], blocks_ref[1, c]
        firsts, seconds = counts
        place_ref[0, firsts] = lax.rem(first, per_dev)
        scale_ref[0, firsts] = 4.0 * weight_ref[c]
        place_ref[1, seconds] = lax.rem(second, per_dev)
        firsts += (lax.div(first, per_dev) == me).astype(jnp.int32)
        seconds += (lax.div(second, per_dev) == me).astype(jnp.int32)
        return firsts, seconds

    if owners == 2 * stride:
        lax.fori_loop(0, blocks_ref.shape[1], mated, jnp.int32(0))
    else:
        lax.fori_loop(0, blocks_ref.shape[1], one, (jnp.int32(0), jnp.int32(0)))


def gather(decoder_ref, blocks, outs, sizes, sem):
    copies = []
    for size, out in zip(sizes, outs):
        for j in range(size):
            copies.append(
                pltpu.make_async_copy(
                    column(decoder_ref, blocks[len(copies)]), column(out, j), sem.at[len(copies)]
                )
            )
            copies[-1].start()
    for copy in copies:
        copy.wait()


def opening_kernel(per_dev, stride, sizes, blocks_ref, decoder_ref, out_ref, held_ref, sem):
    me, owners = lax.axis_index("outer"), lax.axis_size("outer")
    half = per_dev // 2

    def fetch():
        copy = pltpu.make_async_copy(blocks_ref, held_ref, sem.at[0])
        copy.start()
        copy.wait()

    if owners == 2 * stride:

        @pl.when(me >= stride)
        def _():
            copy = pltpu.make_async_copy(decoder_ref.at[:, pl.ds(0, sizes[0] * BLOCK)], out_ref, sem.at[0])
            copy.start()
            copy.wait()

        @pl.when(me < stride)
        def _():
            fetch()
            copies = []
            for j in range(sizes[0]):
                wanted = (me + stride) * per_dev + half + j
                mate = jnp.int32(0)
                for c in range(held_ref.shape[1]):
                    first, second = held_ref[0, c], held_ref[1, c]
                    mate = jnp.where(first == wanted, second, jnp.where(second == wanted, first, mate))
                copies.append(
                    pltpu.make_async_copy(column(decoder_ref, lax.rem(mate, per_dev)), column(out_ref, j), sem.at[j])
                )
                copies[-1].start()
            for copy in copies:
                copy.wait()

    else:
        fetch()
        blocks, c = [], jnp.int32(0)
        for _ in range(sizes[0]):
            c = lax.while_loop(lambda c: lax.div(held_ref[1, c], per_dev) != me, lambda c: c + 1, c)
            blocks.append(lax.rem(held_ref[1, c], per_dev))
            c += 1
        gather(decoder_ref, blocks, [out_ref], sizes, sem)


def planning_kernel(per_dev, stride, start, sizes, blocks_ref, weight_ref, decoder_ref, first_ref, place_ref, scale_ref, *rest):
    outs, sem = rest[:-1], rest[-1]
    plan(per_dev, stride, blocks_ref, weight_ref, place_ref, scale_ref)
    gather(decoder_ref, [place_ref[1, start + j] for j in range(sum(sizes))], outs, sizes, sem)


def gram_parts(x):
    gram = lax.dot_general(x, x, (((0,), (0,)), ((), ())), preferred_element_type=jnp.float32)
    row = lax.broadcasted_iota(jnp.int32, (BLOCK, BLOCK), 0)
    col = lax.broadcasted_iota(jnp.int32, (BLOCK, BLOCK), 1)
    own = jnp.where(row < col, gram[:BLOCK, :BLOCK], gram[BLOCK:, BLOCK:])
    return own, gram[:BLOCK, BLOCK:]


def tangents(x, own, cross, scale):
    row = lax.broadcasted_iota(jnp.int32, (BLOCK, BLOCK), 0)
    col = lax.broadcasted_iota(jnp.int32, (BLOCK, BLOCK), 1)
    upper = jnp.where(row < col, own, 0.0)
    lower = jnp.where(row > col, own, 0.0)
    gram = jnp.concatenate(
        [
            jnp.concatenate([upper + upper.T, cross], axis=1),
            jnp.concatenate([cross.T, lower + lower.T], axis=1),
        ],
        axis=0,
    )
    coef = (gram * scale).astype(jnp.bfloat16)
    along = jnp.sum(gram * coef.astype(jnp.float32), axis=0, keepdims=True)
    grad = jnp.dot(x, coef, preferred_element_type=jnp.float32).astype(jnp.bfloat16)
    return (grad.astype(jnp.float32) - along * x.astype(jnp.float32)).astype(jnp.bfloat16)


def step_kernel(spec, *refs):
    refs = list(refs)
    take = lambda: refs.pop(0)
    place_ref = take()
    scale_ref, decoder_ref = (None, None) if spec["lean"] else (take(), take())
    gram_in = take() if spec["gram"] else None
    final_in = take() if spec["final"] else None
    parts = [take() for _ in range(spec["ranks"])] if spec["final"] else None
    back_in = take() if spec["back"] else None
    for _ in range(spec["unread"]):
        take()
    gram_out = take() if spec["gram"] else None
    send_outs = [take() for _ in range(spec["sends"])]
    out_ref = take() if spec["final"] or spec["back"] else None
    gram_x, final_x, final_t, load_sem, move_sem, store_sem = (None,) * 4 + (refs[0], None) if spec["lean"] else refs

    loads = {}

    def load(kind, scratch, source, start, size):
        for j in range(size):
            pair = (
                pltpu.make_async_copy(
                    column(decoder_ref, place_ref[0, start + j]),
                    scratch.at[j, :, pl.ds(0, BLOCK)],
                    load_sem.at[len(loads), 0],
                ),
                pltpu.make_async_copy(
                    column(source, j), scratch.at[j, :, pl.ds(BLOCK, BLOCK)], load_sem.at[len(loads), 1]
                ),
            )
            for copy in pair:
                copy.start()
            loads[kind, j] = pair

    moves = []

    def move(source, target):
        moves.append(pltpu.make_async_copy(source, target, move_sem.at[len(moves)]))
        moves[-1].start()

    if spec["pack"]:
        start, size = spec["pack"]
        for j in range(size):
            move(column(decoder_ref, place_ref[1, start + j]), column(send_outs[0], j))
    if spec["gram"]:
        load("gram", gram_x, gram_in, *spec["gram"])
    if spec["final"]:
        load("final", final_x, final_in, *spec["final"])
    if spec["back"]:
        start, size = spec["back"]
        for j in range(size):
            move(column(back_in, j), column(out_ref, place_ref[1, start + j]))

    if spec["gram"]:
        for j in range(spec["gram"][1]):
            for copy in loads["gram", j]:
                copy.wait()
            gram_out[j, 0], gram_out[j, 1] = gram_parts(gram_x[j])

    stores = []
    if spec["final"]:
        start, size = spec["final"]
        for j in range(size):
            for copy in loads["final", j]:
                copy.wait()
            a, b, c, d = (part[j] for part in parts)
            total = (a + b) + (c + d)
            final_t[j] = tangents(final_x[j], total[0], total[1], scale_ref[0, start + j])
            everything = (0, final_t.shape[1])
            targets = [(column(out_ref, place_ref[0, start + j]), 0, everything)]
            if spec["pieces"]:
                targets += [
                    (out, BLOCK, rows) for out, (block, rows) in zip(send_outs, spec["pieces"]) if block == j
                ]
            else:
                targets.append((column(send_outs[0], j), BLOCK, everything))
            for target, side, rows in targets:
                stores.append(
                    pltpu.make_async_copy(
                        final_t.at[j, pl.ds(*rows), pl.ds(side, BLOCK)], target, store_sem.at[len(stores)]
                    )
                )
                stores[-1].start()
    for copy in moves + stores:
        copy.wait()


def shards(decoder, stretch_blocks, stretch_weight):
    width, columns = decoder.shape
    per_dev = columns // BLOCK
    half = per_dev // 2
    owners, ranks = lax.axis_size("outer"), lax.axis_size("inner")
    stride = min(owners, per_dev) // 2
    sizes = CHUNKS
    count = len(sizes)
    starts = [sum(sizes[:k]) for k in range(count)]
    chunk = lambda k: (starts[k], sizes[k])
    array = lambda k: jax.ShapeDtypeStruct((width, sizes[k] * BLOCK), decoder.dtype)
    out_shape = jax.ShapeDtypeStruct(decoder.shape, decoder.dtype)
    to_first = [(o, (o + stride) % owners) for o in range(owners)]
    to_second = [(o, (o - stride) % owners) for o in range(owners)]

    stay = lambda x: pltpu.with_memory_space_constraint(x, pltpu.HBM)
    pairs, decoder = stay(stretch_blocks.T), stay(decoder)
    first = pl.pallas_call(
        functools.partial(opening_kernel, per_dev, stride, sizes[:1]),
        out_shape=array(0),
        in_specs=[HBM, HBM],
        out_specs=ANY,
        scratch_shapes=[pltpu.SMEM(pairs.shape, jnp.int32), pltpu.SemaphoreType.DMA((sizes[0],))],
        compiler_params=pltpu.CompilerParams(vmem_limit_bytes=8 * 2**20),
        name="opening",
    )(pairs, decoder)
    place, scale, *raw = pl.pallas_call(
        functools.partial(planning_kernel, per_dev, stride, starts[1], sizes[1:LAG]),
        out_shape=[
            jax.ShapeDtypeStruct((2, half + 1), jnp.int32),
            jax.ShapeDtypeStruct((1, half + 1), jnp.float32),
        ]
        + [array(k) for k in range(1, LAG)],
        in_specs=[SMEM, SMEM, HBM, ANY],
        out_specs=[SMEM, SMEM] + [ANY] * (LAG - 1),
        scratch_shapes=[pltpu.SemaphoreType.DMA((per_dev,))],
        compiler_params=pltpu.CompilerParams(vmem_limit_bytes=8 * 2**20),
        name="planning",
    )(pairs, stay(stretch_weight), decoder, first)

    sends = [lax.ppermute(part, "outer", to_first) for part in [first] + raw]
    last = width // LAST
    pieces = [(j, (0, width)) for j in range(sizes[-1] - 1)]
    pieces += [(sizes[-1] - 1, (0, width - last)), (sizes[-1] - 1, (width - last, last))]
    parts = {}
    out = chain = None
    for step in range(2 * count - 1):
        arrived = sends[step]
        gram = chunk(step) if step < count else None
        pack = chunk(step + LAG) if step + LAG < count else None
        turn = step + LAG - count
        final = chunk(turn) if 0 <= turn < count else None
        back = chunk(step - count) if step >= count else None
        spec = {"gram": gram, "pack": pack, "final": final, "back": back, "ranks": ranks, "unread": 0}
        spec["lean"] = not (gram or pack or final)
        args, specs = [place], [SMEM]
        if not spec["lean"]:
            args, specs = args + [scale, decoder], specs + [SMEM, HBM]
        shapes, out_specs, aliases = [], [], {}
        if gram:
            args, specs = args + [arrived], specs + [ANY]
            shapes.append(jax.ShapeDtypeStruct((gram[1], 2, BLOCK, BLOCK), jnp.float32))
            out_specs.append(VMEM)
        if final:
            args, specs = args + [sends[turn]] + parts.pop(turn), specs + [ANY] + [VMEM] * ranks
        if back:
            args, specs = args + [arrived], specs + [ANY]
        spec["sends"], spec["pieces"] = int(bool(final or pack)), None
        if turn == count - 1:
            spec["sends"], spec["pieces"] = len(pieces), pieces
            shapes += [jax.ShapeDtypeStruct((size, BLOCK), decoder.dtype) for _, (_, size) in pieces]
            out_specs += [ANY] * len(pieces)
        elif final or pack:
            shapes.append(array(turn if final else step + LAG))
            out_specs.append(ANY)
        if final or back:
            if out is not None:
                aliases = {len(args): len(shapes)}
                args, specs, chain = args + [out], specs + [ANY], None
                spec["unread"] += 1
            shapes.append(out_shape)
            out_specs.append(ANY)
        if chain is not None:
            args, specs = args + [chain], specs + [ANY]
            spec["unread"] += 1
        slot = max(sizes)
        results = list(
            pl.pallas_call(
                functools.partial(step_kernel, spec),
                out_shape=shapes,
                in_specs=specs,
                out_specs=out_specs,
                input_output_aliases=aliases,
                scratch_shapes=[pltpu.SemaphoreType.DMA((2 * slot,))]
                if spec["lean"]
                else [
                    pltpu.VMEM((slot, width, STRETCH), decoder.dtype),
                    pltpu.VMEM((slot, width, STRETCH), decoder.dtype),
                    pltpu.VMEM((slot, width, STRETCH), decoder.dtype),
                    pltpu.SemaphoreType.DMA((2 * slot, 2)),
                    pltpu.SemaphoreType.DMA((2 * slot,)),
                    pltpu.SemaphoreType.DMA((2 * slot + 1,)),
                ],
                compiler_params=pltpu.CompilerParams(vmem_limit_bytes=32 * 2**20),
                name="step",
            )(*args)
        )
        if gram:
            chain = mine = results.pop(0)
            parts[step] = [mine] + [
                lax.ppermute(mine, "inner", [(i, i ^ hop) for i in range(ranks)]) for hop in range(1, ranks)
            ]
        for _ in range(spec["sends"]):
            sends.append(lax.ppermute(results.pop(0), "outer", to_second if final else to_first))
        if final or back:
            out = results.pop(0)
    for piece, (block, rows) in zip(sends[-len(pieces) :], pieces):
        out = lax.dynamic_update_slice(out, piece, (rows[0], place[1, starts[-1] + block] * BLOCK))
    return out


def solution(mesh):
    placed = (P("inner", ("groups", "outer")), P("groups", None), P("groups"))
    return jax.shard_map(
        shards,
        mesh=mesh,
        in_specs=placed,
        out_specs=P("inner", ("groups", "outer")),
        check_vma=False,
    )
```

```python
import functools

import jax
import jax.numpy as jnp
from jax import lax
from jax.experimental import pallas as pl
from jax.experimental.pallas import tpu as pltpu
from jax.sharding import PartitionSpec as P

BLOCK = 128
STRETCH = 256
CHUNKS = (2, 2, 2, 2)
LAST = 4
LAG = 2

ANY = pl.BlockSpec(memory_space=pl.ANY)
HBM = pl.BlockSpec(memory_space=pltpu.HBM)
VMEM = pl.BlockSpec(memory_space=pltpu.VMEM)
SMEM = pl.BlockSpec(memory_space=pltpu.SMEM)


def column(ref, block):
    start = block * BLOCK
    if not isinstance(block, int):
        start = pl.multiple_of(start, BLOCK)
    return ref.at[:, pl.ds(start, BLOCK)]


def plan(per_dev, stride, blocks_ref, weight_ref, place_ref, scale_ref):
    me, owners = lax.axis_index("outer"), lax.axis_size("outer")
    half = per_dev // 2

    def mated(c, carry):
        first, second = blocks_ref[0, c], blocks_ref[1, c]
        first_mine = lax.div(first, per_dev) == me
        mine = jnp.where(first_mine, first, second)
        other = lax.rem(jnp.where(first_mine, second, first), per_dev)
        upper = me >= stride
        local = lax.rem(mine, per_dev)
        key = jnp.where(upper, local, other)
        spare = lax.div(mine, per_dev) != me
        keeps = (key >= half) == upper
        slot = lax.rem(key, half)
        kept = jnp.where(spare | jnp.logical_not(keeps), half, slot)
        place_ref[0, kept] = local
        scale_ref[0, kept] = 4.0 * weight_ref[c]
        place_ref[1, jnp.where(spare | keeps, half, slot)] = local
        return carry

    def one(c, counts):
        first, second = blocks_ref[0, c], blocks_ref[1, c]
        firsts, seconds = counts
        place_ref[0, firsts] = lax.rem(first, per_dev)
        scale_ref[0, firsts] = 4.0 * weight_ref[c]
        place_ref[1, seconds] = lax.rem(second, per_dev)
        firsts += (lax.div(first, per_dev) == me).astype(jnp.int32)
        seconds += (lax.div(second, per_dev) == me).astype(jnp.int32)
        return firsts, seconds

    if owners == 2 * stride:
        lax.fori_loop(0, blocks_ref.shape[1], mated, jnp.int32(0))
    else:
        lax.fori_loop(0, blocks_ref.shape[1], one, (jnp.int32(0), jnp.int32(0)))


def gather(decoder_ref, blocks, outs, sizes, sem):
    copies = []
    for size, out in zip(sizes, outs):
        for j in range(size):
            copies.append(
                pltpu.make_async_copy(
                    column(decoder_ref, blocks[len(copies)]), column(out, j), sem.at[len(copies)]
                )
            )
            copies[-1].start()
    for copy in copies:
        copy.wait()


def opening_kernel(per_dev, stride, sizes, blocks_ref, decoder_ref, out_ref, held_ref, sem):
    me, owners = lax.axis_index("outer"), lax.axis_size("outer")
    half = per_dev // 2

    def fetch():
        copy = pltpu.make_async_copy(blocks_ref, held_ref, sem.at[0])
        copy.start()
        copy.wait()

    if owners == 2 * stride:

        @pl.when(me >= stride)
        def _():
            gather(decoder_ref, range(sizes[0]), [out_ref], sizes, sem)

        @pl.when(me < stride)
        def _():
            fetch()
            copies = []
            for j in range(sizes[0]):
                wanted = (me + stride) * per_dev + half + j
                mate = jnp.int32(0)
                for c in range(held_ref.shape[1]):
                    first, second = held_ref[0, c], held_ref[1, c]
                    mate = jnp.where(first == wanted, second, jnp.where(second == wanted, first, mate))
                copies.append(
                    pltpu.make_async_copy(column(decoder_ref, lax.rem(mate, per_dev)), column(out_ref, j), sem.at[j])
                )
                copies[-1].start()
            for copy in copies:
                copy.wait()

    else:
        fetch()
        blocks, c = [], jnp.int32(0)
        for _ in range(sizes[0]):
            c = lax.while_loop(lambda c: lax.div(held_ref[1, c], per_dev) != me, lambda c: c + 1, c)
            blocks.append(lax.rem(held_ref[1, c], per_dev))
            c += 1
        gather(decoder_ref, blocks, [out_ref], sizes, sem)


def planning_kernel(per_dev, stride, start, sizes, blocks_ref, weight_ref, decoder_ref, first_ref, place_ref, scale_ref, *rest):
    outs, sem = rest[:-1], rest[-1]
    plan(per_dev, stride, blocks_ref, weight_ref, place_ref, scale_ref)
    gather(decoder_ref, [place_ref[1, start + j] for j in range(sum(sizes))], outs, sizes, sem)


def gram_parts(x):
    gram = lax.dot_general(x, x, (((0,), (0,)), ((), ())), preferred_element_type=jnp.float32)
    row = lax.broadcasted_iota(jnp.int32, (BLOCK, BLOCK), 0)
    col = lax.broadcasted_iota(jnp.int32, (BLOCK, BLOCK), 1)
    own = jnp.where(row < col, gram[:BLOCK, :BLOCK], gram[BLOCK:, BLOCK:])
    return own, gram[:BLOCK, BLOCK:]


def tangents(x, own, cross, scale):
    row = lax.broadcasted_iota(jnp.int32, (BLOCK, BLOCK), 0)
    col = lax.broadcasted_iota(jnp.int32, (BLOCK, BLOCK), 1)
    upper = jnp.where(row < col, own, 0.0)
    lower = jnp.where(row > col, own, 0.0)
    gram = jnp.concatenate(
        [
            jnp.concatenate([upper + upper.T, cross], axis=1),
            jnp.concatenate([cross.T, lower + lower.T], axis=1),
        ],
        axis=0,
    )
    coef = (gram * scale).astype(jnp.bfloat16)
    along = jnp.sum(gram * coef.astype(jnp.float32), axis=0, keepdims=True)
    grad = jnp.dot(x, coef, preferred_element_type=jnp.float32).astype(jnp.bfloat16)
    return (grad.astype(jnp.float32) - along * x.astype(jnp.float32)).astype(jnp.bfloat16)


def step_kernel(spec, *refs):
    refs = list(refs)
    take = lambda: refs.pop(0)
    place_ref = take()
    scale_ref, decoder_ref = (None, None) if spec["lean"] else (take(), take())
    gram_in = take() if spec["gram"] else None
    final_in = take() if spec["final"] else None
    parts = [take() for _ in range(spec["ranks"])] if spec["final"] else None
    back_in = take() if spec["back"] else None
    for _ in range(spec["unread"]):
        take()
    gram_out = take() if spec["gram"] else None
    send_outs = [take() for _ in range(spec["sends"])]
    out_ref = take() if spec["final"] or spec["back"] else None
    gram_x, final_x, final_t, load_sem, move_sem, store_sem = (None,) * 4 + (refs[0], None) if spec["lean"] else refs

    loads = {}

    def load(kind, scratch, source, start, size):
        for j in range(size):
            pair = (
                pltpu.make_async_copy(
                    column(decoder_ref, place_ref[0, start + j]),
                    scratch.at[j, :, pl.ds(0, BLOCK)],
                    load_sem.at[len(loads), 0],
                ),
                pltpu.make_async_copy(
                    column(source, j), scratch.at[j, :, pl.ds(BLOCK, BLOCK)], load_sem.at[len(loads), 1]
                ),
            )
            for copy in pair:
                copy.start()
            loads[kind, j] = pair

    moves = []

    def move(source, target):
        moves.append(pltpu.make_async_copy(source, target, move_sem.at[len(moves)]))
        moves[-1].start()

    if spec["pack"]:
        start, size = spec["pack"]
        for j in range(size):
            move(column(decoder_ref, place_ref[1, start + j]), column(send_outs[0], j))
    if spec["gram"]:
        load("gram", gram_x, gram_in, *spec["gram"])
    if spec["final"]:
        load("final", final_x, final_in, *spec["final"])
    if spec["back"]:
        start, size = spec["back"]
        for j in range(size):
            move(column(back_in, j), column(out_ref, place_ref[1, start + j]))

    if spec["gram"]:
        for j in range(spec["gram"][1]):
            for copy in loads["gram", j]:
                copy.wait()
            gram_out[j, 0], gram_out[j, 1] = gram_parts(gram_x[j])

    stores = []
    if spec["final"]:
        start, size = spec["final"]
        for j in range(size):
            for copy in loads["final", j]:
                copy.wait()
            a, b, c, d = (part[j] for part in parts)
            total = (a + b) + (c + d)
            final_t[j] = tangents(final_x[j], total[0], total[1], scale_ref[0, start + j])
            everything = (0, final_t.shape[1])
            targets = [(column(out_ref, place_ref[0, start + j]), 0, everything)]
            if spec["pieces"]:
                targets += [
                    (out, BLOCK, rows) for out, (block, rows) in zip(send_outs, spec["pieces"]) if block == j
                ]
            else:
                targets.append((column(send_outs[0], j), BLOCK, everything))
            for target, side, rows in targets:
                stores.append(
                    pltpu.make_async_copy(
                        final_t.at[j, pl.ds(*rows), pl.ds(side, BLOCK)], target, store_sem.at[len(stores)]
                    )
                )
                stores[-1].start()
    for copy in moves + stores:
        copy.wait()


def shards(decoder, stretch_blocks, stretch_weight):
    width, columns = decoder.shape
    per_dev = columns // BLOCK
    half = per_dev // 2
    owners, ranks = lax.axis_size("outer"), lax.axis_size("inner")
    stride = min(owners, per_dev) // 2
    sizes = CHUNKS
    count = len(sizes)
    starts = [sum(sizes[:k]) for k in range(count)]
    chunk = lambda k: (starts[k], sizes[k])
    array = lambda k: jax.ShapeDtypeStruct((width, sizes[k] * BLOCK), decoder.dtype)
    out_shape = jax.ShapeDtypeStruct(decoder.shape, decoder.dtype)
    to_first = [(o, (o + stride) % owners) for o in range(owners)]
    to_second = [(o, (o - stride) % owners) for o in range(owners)]

    stay = lambda x: pltpu.with_memory_space_constraint(x, pltpu.HBM)
    pairs, decoder = stay(stretch_blocks.T), stay(decoder)
    first = pl.pallas_call(
        functools.partial(opening_kernel, per_dev, stride, sizes[:1]),
        out_shape=array(0),
        in_specs=[HBM, HBM],
        out_specs=ANY,
        scratch_shapes=[pltpu.SMEM(pairs.shape, jnp.int32), pltpu.SemaphoreType.DMA((sizes[0],))],
        compiler_params=pltpu.CompilerParams(vmem_limit_bytes=8 * 2**20),
        name="opening",
    )(pairs, decoder)
    place, scale, *raw = pl.pallas_call(
        functools.partial(planning_kernel, per_dev, stride, starts[1], sizes[1:LAG]),
        out_shape=[
            jax.ShapeDtypeStruct((2, half + 1), jnp.int32),
            jax.ShapeDtypeStruct((1, half + 1), jnp.float32),
        ]
        + [array(k) for k in range(1, LAG)],
        in_specs=[SMEM, SMEM, HBM, ANY],
        out_specs=[SMEM, SMEM] + [ANY] * (LAG - 1),
        scratch_shapes=[pltpu.SemaphoreType.DMA((per_dev,))],
        compiler_params=pltpu.CompilerParams(vmem_limit_bytes=8 * 2**20),
        name="planning",
    )(pairs, stay(stretch_weight), decoder, first)

    sends = [lax.ppermute(part, "outer", to_first) for part in [first] + raw]
    last = width // LAST
    pieces = [(j, (0, width)) for j in range(sizes[-1] - 1)]
    pieces += [(sizes[-1] - 1, (0, width - last)), (sizes[-1] - 1, (width - last, last))]
    parts = {}
    out = chain = None
    for step in range(2 * count - 1):
        arrived = sends[step]
        gram = chunk(step) if step < count else None
        pack = chunk(step + LAG) if step + LAG < count else None
        turn = step + LAG - count
        final = chunk(turn) if 0 <= turn < count else None
        back = chunk(step - count) if step >= count else None
        spec = {"gram": gram, "pack": pack, "final": final, "back": back, "ranks": ranks, "unread": 0}
        spec["lean"] = not (gram or pack or final)
        args, specs = [place], [SMEM]
        if not spec["lean"]:
            args, specs = args + [scale, decoder], specs + [SMEM, HBM]
        shapes, out_specs, aliases = [], [], {}
        if gram:
            args, specs = args + [arrived], specs + [ANY]
            shapes.append(jax.ShapeDtypeStruct((gram[1], 2, BLOCK, BLOCK), jnp.float32))
            out_specs.append(VMEM)
        if final:
            args, specs = args + [sends[turn]] + parts.pop(turn), specs + [ANY] + [VMEM] * ranks
        if back:
            args, specs = args + [arrived], specs + [ANY]
        spec["sends"], spec["pieces"] = int(bool(final or pack)), None
        if turn == count - 1:
            spec["sends"], spec["pieces"] = len(pieces), pieces
            shapes += [jax.ShapeDtypeStruct((size, BLOCK), decoder.dtype) for _, (_, size) in pieces]
            out_specs += [ANY] * len(pieces)
        elif final or pack:
            shapes.append(array(turn if final else step + LAG))
            out_specs.append(ANY)
        if final or back:
            if out is not None:
                aliases = {len(args): len(shapes)}
                args, specs, chain = args + [out], specs + [ANY], None
                spec["unread"] += 1
            shapes.append(out_shape)
            out_specs.append(ANY)
        if chain is not None:
            args, specs = args + [chain], specs + [ANY]
            spec["unread"] += 1
        slot = max(sizes)
        results = list(
            pl.pallas_call(
                functools.partial(step_kernel, spec),
                out_shape=shapes,
                in_specs=specs,
                out_specs=out_specs,
                input_output_aliases=aliases,
                scratch_shapes=[pltpu.SemaphoreType.DMA((2 * slot,))]
                if spec["lean"]
                else [
                    pltpu.VMEM((slot, width, STRETCH), decoder.dtype),
                    pltpu.VMEM((slot, width, STRETCH), decoder.dtype),
                    pltpu.VMEM((slot, width, STRETCH), decoder.dtype),
                    pltpu.SemaphoreType.DMA((2 * slot, 2)),
                    pltpu.SemaphoreType.DMA((2 * slot,)),
                    pltpu.SemaphoreType.DMA((2 * slot + 1,)),
                ],
                compiler_params=pltpu.CompilerParams(vmem_limit_bytes=32 * 2**20),
                name="step",
            )(*args)
        )
        if gram:
            chain = mine = results.pop(0)
            parts[step] = [mine] + [
                lax.ppermute(mine, "inner", [(i, i ^ hop) for i in range(ranks)]) for hop in range(1, ranks)
            ]
        for _ in range(spec["sends"]):
            sends.append(lax.ppermute(results.pop(0), "outer", to_second if final else to_first))
        if final or back:
            out = results.pop(0)
    for piece, (block, rows) in zip(sends[-len(pieces) :], pieces):
        out = lax.dynamic_update_slice(out, piece, (rows[0], place[1, starts[-1] + block] * BLOCK))
    return out


def solution(mesh):
    placed = (P("inner", ("groups", "outer")), P("groups", None), P("groups"))
    return jax.shard_map(
        shards,
        mesh=mesh,
        in_specs=placed,
        out_specs=P("inner", ("groups", "outer")),
        check_vma=False,
    )
```

```python
import functools

import jax
import jax.numpy as jnp
from jax import lax
from jax.experimental import pallas as pl
from jax.experimental.pallas import tpu as pltpu
from jax.sharding import PartitionSpec as P

BLOCK = 128
STRETCH = 256
CHUNKS = (2, 2, 2, 2)
LAST = 2
LAG = 2

ANY = pl.BlockSpec(memory_space=pl.ANY)
HBM = pl.BlockSpec(memory_space=pltpu.HBM)
VMEM = pl.BlockSpec(memory_space=pltpu.VMEM)
SMEM = pl.BlockSpec(memory_space=pltpu.SMEM)


def column(ref, block):
    start = block * BLOCK
    if not isinstance(block, int):
        start = pl.multiple_of(start, BLOCK)
    return ref.at[:, pl.ds(start, BLOCK)]


def plan(per_dev, stride, blocks_ref, weight_ref, place_ref, scale_ref):
    me, owners = lax.axis_index("outer"), lax.axis_size("outer")
    half = per_dev // 2

    def mated(c, carry):
        first, second = blocks_ref[0, c], blocks_ref[1, c]
        first_mine = lax.div(first, per_dev) == me
        mine = jnp.where(first_mine, first, second)
        other = lax.rem(jnp.where(first_mine, second, first), per_dev)
        upper = me >= stride
        local = lax.rem(mine, per_dev)
        key = jnp.where(upper, local, other)
        spare = lax.div(mine, per_dev) != me
        keeps = (key >= half) == upper
        slot = lax.rem(key, half)
        kept = jnp.where(spare | jnp.logical_not(keeps), half, slot)
        place_ref[0, kept] = local
        scale_ref[0, kept] = 4.0 * weight_ref[c]
        place_ref[1, jnp.where(spare | keeps, half, slot)] = local
        return carry

    def one(c, counts):
        first, second = blocks_ref[0, c], blocks_ref[1, c]
        firsts, seconds = counts
        place_ref[0, firsts] = lax.rem(first, per_dev)
        scale_ref[0, firsts] = 4.0 * weight_ref[c]
        place_ref[1, seconds] = lax.rem(second, per_dev)
        firsts += (lax.div(first, per_dev) == me).astype(jnp.int32)
        seconds += (lax.div(second, per_dev) == me).astype(jnp.int32)
        return firsts, seconds

    if owners == 2 * stride:
        lax.fori_loop(0, blocks_ref.shape[1], mated, jnp.int32(0))
    else:
        lax.fori_loop(0, blocks_ref.shape[1], one, (jnp.int32(0), jnp.int32(0)))


def gather(decoder_ref, blocks, outs, sizes, sem):
    copies = []
    for size, out in zip(sizes, outs):
        for j in range(size):
            copies.append(
                pltpu.make_async_copy(
                    column(decoder_ref, blocks[len(copies)]), column(out, j), sem.at[len(copies)]
                )
            )
            copies[-1].start()
    for copy in copies:
        copy.wait()


def opening_kernel(per_dev, stride, sizes, blocks_ref, decoder_ref, out_ref, held_ref, sem):
    me, owners = lax.axis_index("outer"), lax.axis_size("outer")
    half = per_dev // 2

    def fetch():
        copy = pltpu.make_async_copy(blocks_ref, held_ref, sem.at[0])
        copy.start()
        copy.wait()

    if owners == 2 * stride:

        @pl.when(me >= stride)
        def _():
            gather(decoder_ref, range(sizes[0]), [out_ref], sizes, sem)

        @pl.when(me < stride)
        def _():
            fetch()
            copies = []
            for j in range(sizes[0]):
                wanted = (me + stride) * per_dev + half + j
                mate = jnp.int32(0)
                for c in range(held_ref.shape[1]):
                    first, second = held_ref[0, c], held_ref[1, c]
                    mate = jnp.where(first == wanted, second, jnp.where(second == wanted, first, mate))
                copies.append(
                    pltpu.make_async_copy(column(decoder_ref, lax.rem(mate, per_dev)), column(out_ref, j), sem.at[j])
                )
                copies[-1].start()
            for copy in copies:
                copy.wait()

    else:
        fetch()
        blocks, c = [], jnp.int32(0)
        for _ in range(sizes[0]):
            c = lax.while_loop(lambda c: lax.div(held_ref[1, c], per_dev) != me, lambda c: c + 1, c)
            blocks.append(lax.rem(held_ref[1, c], per_dev))
            c += 1
        gather(decoder_ref, blocks, [out_ref], sizes, sem)


def planning_kernel(per_dev, stride, start, sizes, blocks_ref, weight_ref, decoder_ref, first_ref, place_ref, scale_ref, *rest):
    outs, sem = rest[:-1], rest[-1]
    plan(per_dev, stride, blocks_ref, weight_ref, place_ref, scale_ref)
    gather(decoder_ref, [place_ref[1, start + j] for j in range(sum(sizes))], outs, sizes, sem)


def gram_parts(x):
    gram = lax.dot_general(x, x, (((0,), (0,)), ((), ())), preferred_element_type=jnp.float32)
    row = lax.broadcasted_iota(jnp.int32, (BLOCK, BLOCK), 0)
    col = lax.broadcasted_iota(jnp.int32, (BLOCK, BLOCK), 1)
    own = jnp.where(row < col, gram[:BLOCK, :BLOCK], gram[BLOCK:, BLOCK:])
    return own, gram[:BLOCK, BLOCK:]


def tangents(x, own, cross, scale):
    row = lax.broadcasted_iota(jnp.int32, (BLOCK, BLOCK), 0)
    col = lax.broadcasted_iota(jnp.int32, (BLOCK, BLOCK), 1)
    upper = jnp.where(row < col, own, 0.0)
    lower = jnp.where(row > col, own, 0.0)
    gram = jnp.concatenate(
        [
            jnp.concatenate([upper + upper.T, cross], axis=1),
            jnp.concatenate([cross.T, lower + lower.T], axis=1),
        ],
        axis=0,
    )
    coef = (gram * scale).astype(jnp.bfloat16)
    along = jnp.sum(gram * coef.astype(jnp.float32), axis=0, keepdims=True)
    grad = jnp.dot(x, coef, preferred_element_type=jnp.float32).astype(jnp.bfloat16)
    return (grad.astype(jnp.float32) - along * x.astype(jnp.float32)).astype(jnp.bfloat16)


def step_kernel(spec, *refs):
    refs = list(refs)
    take = lambda: refs.pop(0)
    place_ref = take()
    scale_ref, decoder_ref = (None, None) if spec["lean"] else (take(), take())
    gram_in = take() if spec["gram"] else None
    final_in = take() if spec["final"] else None
    parts = [take() for _ in range(spec["ranks"])] if spec["final"] else None
    back_in = take() if spec["back"] else None
    for _ in range(spec["unread"]):
        take()
    gram_out = take() if spec["gram"] else None
    send_outs = [take() for _ in range(spec["sends"])]
    out_ref = take() if spec["final"] or spec["back"] else None
    gram_x, final_x, final_t, load_sem, move_sem, store_sem = (None,) * 4 + (refs[0], None) if spec["lean"] else refs

    loads = {}

    def load(kind, scratch, source, start, size):
        for j in range(size):
            pair = (
                pltpu.make_async_copy(
                    column(decoder_ref, place_ref[0, start + j]),
                    scratch.at[j, :, pl.ds(0, BLOCK)],
                    load_sem.at[len(loads), 0],
                ),
                pltpu.make_async_copy(
                    column(source, j), scratch.at[j, :, pl.ds(BLOCK, BLOCK)], load_sem.at[len(loads), 1]
                ),
            )
            for copy in pair:
                copy.start()
            loads[kind, j] = pair

    moves = []

    def move(source, target):
        moves.append(pltpu.make_async_copy(source, target, move_sem.at[len(moves)]))
        moves[-1].start()

    if spec["pack"]:
        start, size = spec["pack"]
        for j in range(size):
            move(column(decoder_ref, place_ref[1, start + j]), column(send_outs[0], j))
    if spec["gram"]:
        load("gram", gram_x, gram_in, *spec["gram"])
    if spec["final"]:
        load("final", final_x, final_in, *spec["final"])
    if spec["back"]:
        start, size = spec["back"]
        for j in range(size):
            move(column(back_in, j), column(out_ref, place_ref[1, start + j]))

    if spec["gram"]:
        for j in range(spec["gram"][1]):
            for copy in loads["gram", j]:
                copy.wait()
            gram_out[j, 0], gram_out[j, 1] = gram_parts(gram_x[j])

    stores = []
    if spec["final"]:
        start, size = spec["final"]
        for j in range(size):
            for copy in loads["final", j]:
                copy.wait()
            a, b, c, d = (part[j] for part in parts)
            total = (a + b) + (c + d)
            final_t[j] = tangents(final_x[j], total[0], total[1], scale_ref[0, start + j])
            everything = (0, final_t.shape[1])
            targets = [(column(out_ref, place_ref[0, start + j]), 0, everything)]
            if spec["pieces"]:
                targets += [
                    (out, BLOCK, rows) for out, (block, rows) in zip(send_outs, spec["pieces"]) if block == j
                ]
            else:
                targets.append((column(send_outs[0], j), BLOCK, everything))
            for target, side, rows in targets:
                stores.append(
                    pltpu.make_async_copy(
                        final_t.at[j, pl.ds(*rows), pl.ds(side, BLOCK)], target, store_sem.at[len(stores)]
                    )
                )
                stores[-1].start()
    for copy in moves + stores:
        copy.wait()


def shards(decoder, stretch_blocks, stretch_weight):
    width, columns = decoder.shape
    per_dev = columns // BLOCK
    half = per_dev // 2
    owners, ranks = lax.axis_size("outer"), lax.axis_size("inner")
    stride = min(owners, per_dev) // 2
    sizes = CHUNKS
    count = len(sizes)
    starts = [sum(sizes[:k]) for k in range(count)]
    chunk = lambda k: (starts[k], sizes[k])
    array = lambda k: jax.ShapeDtypeStruct((width, sizes[k] * BLOCK), decoder.dtype)
    out_shape = jax.ShapeDtypeStruct(decoder.shape, decoder.dtype)
    to_first = [(o, (o + stride) % owners) for o in range(owners)]
    to_second = [(o, (o - stride) % owners) for o in range(owners)]

    stay = lambda x: pltpu.with_memory_space_constraint(x, pltpu.HBM)
    pairs, decoder = stay(stretch_blocks.T), stay(decoder)
    first = pl.pallas_call(
        functools.partial(opening_kernel, per_dev, stride, sizes[:1]),
        out_shape=array(0),
        in_specs=[HBM, HBM],
        out_specs=ANY,
        scratch_shapes=[pltpu.SMEM(pairs.shape, jnp.int32), pltpu.SemaphoreType.DMA((sizes[0],))],
        compiler_params=pltpu.CompilerParams(vmem_limit_bytes=8 * 2**20),
        name="opening",
    )(pairs, decoder)
    place, scale, *raw = pl.pallas_call(
        functools.partial(planning_kernel, per_dev, stride, starts[1], sizes[1:LAG]),
        out_shape=[
            jax.ShapeDtypeStruct((2, half + 1), jnp.int32),
            jax.ShapeDtypeStruct((1, half + 1), jnp.float32),
        ]
        + [array(k) for k in range(1, LAG)],
        in_specs=[SMEM, SMEM, HBM, ANY],
        out_specs=[SMEM, SMEM] + [ANY] * (LAG - 1),
        scratch_shapes=[pltpu.SemaphoreType.DMA((per_dev,))],
        compiler_params=pltpu.CompilerParams(vmem_limit_bytes=8 * 2**20),
        name="planning",
    )(pairs, stay(stretch_weight), decoder, first)

    sends = [lax.ppermute(part, "outer", to_first) for part in [first] + raw]
    last = width // LAST
    pieces = [(j, (0, width)) for j in range(sizes[-1] - 1)]
    pieces += [(sizes[-1] - 1, (0, width - last)), (sizes[-1] - 1, (width - last, last))]
    parts = {}
    out = chain = None
    for step in range(2 * count - 1):
        arrived = sends[step]
        gram = chunk(step) if step < count else None
        pack = chunk(step + LAG) if step + LAG < count else None
        turn = step + LAG - count
        final = chunk(turn) if 0 <= turn < count else None
        back = chunk(step - count) if step >= count else None
        spec = {"gram": gram, "pack": pack, "final": final, "back": back, "ranks": ranks, "unread": 0}
        spec["lean"] = not (gram or pack or final)
        args, specs = [place], [SMEM]
        if not spec["lean"]:
            args, specs = args + [scale, decoder], specs + [SMEM, HBM]
        shapes, out_specs, aliases = [], [], {}
        if gram:
            args, specs = args + [arrived], specs + [ANY]
            shapes.append(jax.ShapeDtypeStruct((gram[1], 2, BLOCK, BLOCK), jnp.float32))
            out_specs.append(VMEM)
        if final:
            args, specs = args + [sends[turn]] + parts.pop(turn), specs + [ANY] + [VMEM] * ranks
        if back:
            args, specs = args + [arrived], specs + [ANY]
        spec["sends"], spec["pieces"] = int(bool(final or pack)), None
        if turn == count - 1:
            spec["sends"], spec["pieces"] = len(pieces), pieces
            shapes += [jax.ShapeDtypeStruct((size, BLOCK), decoder.dtype) for _, (_, size) in pieces]
            out_specs += [ANY] * len(pieces)
        elif final or pack:
            shapes.append(array(turn if final else step + LAG))
            out_specs.append(ANY)
        if final or back:
            if out is not None:
                aliases = {len(args): len(shapes)}
                args, specs, chain = args + [out], specs + [ANY], None
                spec["unread"] += 1
            shapes.append(out_shape)
            out_specs.append(ANY)
        if chain is not None:
            args, specs = args + [chain], specs + [ANY]
            spec["unread"] += 1
        slot = max(sizes)
        results = list(
            pl.pallas_call(
                functools.partial(step_kernel, spec),
                out_shape=shapes,
                in_specs=specs,
                out_specs=out_specs,
                input_output_aliases=aliases,
                scratch_shapes=[pltpu.SemaphoreType.DMA((2 * slot,))]
                if spec["lean"]
                else [
                    pltpu.VMEM((slot, width, STRETCH), decoder.dtype),
                    pltpu.VMEM((slot, width, STRETCH), decoder.dtype),
                    pltpu.VMEM((slot, width, STRETCH), decoder.dtype),
                    pltpu.SemaphoreType.DMA((2 * slot, 2)),
                    pltpu.SemaphoreType.DMA((2 * slot,)),
                    pltpu.SemaphoreType.DMA((2 * slot + 1,)),
                ],
                compiler_params=pltpu.CompilerParams(vmem_limit_bytes=32 * 2**20),
                name="step",
            )(*args)
        )
        if gram:
            chain = mine = results.pop(0)
            parts[step] = [mine] + [
                lax.ppermute(mine, "inner", [(i, i ^ hop) for i in range(ranks)]) for hop in range(1, ranks)
            ]
        for _ in range(spec["sends"]):
            sends.append(lax.ppermute(results.pop(0), "outer", to_second if final else to_first))
        if final or back:
            out = results.pop(0)
    for piece, (block, rows) in zip(sends[-len(pieces) :], pieces):
        out = lax.dynamic_update_slice(out, piece, (rows[0], place[1, starts[-1] + block] * BLOCK))
    return out


def solution(mesh):
    placed = (P("inner", ("groups", "outer")), P("groups", None), P("groups"))
    return jax.shard_map(
        shards,
        mesh=mesh,
        in_specs=placed,
        out_specs=P("inner", ("groups", "outer")),
        check_vma=False,
    )
```
